256 devices in a mesh: group: 8 (over z), dom: 32 (over x, y, core).
Axes of the slice: x: 4, y: 4, z: 8, core: 2. Of those that a mesh axis runs over, the one named last changes fastest.
Arguments:
- query_rows: bfloat16 [196608, 256], P(('group', 'dom')), may hold values from -64 to 64
- key_rows: bfloat16 [196608, 256], P(('group', 'dom')), may hold values from -6 to 6
- value_rows: bfloat16 [196608, 256], P(('group', 'dom')), may hold values from -6 to 6
- out_weight: bfloat16 [256, 256], replicated, may hold values from -1.5 to 1.5
- grad_update: bfloat16 [196608, 256], P(('group', 'dom')), may hold values from -6 to 6
- expander_bias: float32 [8], replicated, may hold values from 1 to 5
- tile_block: int32 [256, 6, 8], P(('group', 'dom')), may hold values from 0 to 37, as said below
- tile_count: int32 [256, 6], P(('group', 'dom')), may hold values from 5 to 8, as said below
- send_block: int32 [256, 32], P(('group', 'dom')), may hold values from 0 to 5
- matching: int32 [256, 3, 768], P(('group', 'dom')), may hold values from 0 to 767, each once within a row
Outputs:
- update: bfloat16 [196608, 256], P(('group', 'dom'))
- query_grad: float32 [196608, 256], P(('group', 'dom'))
- key_grad: float32 [196608, 256], P(('group', 'dom'))
- value_grad: float32 [196608, 256], P(('group', 'dom'))
- weight_grad: float32 [256, 256], replicated
The draws below stay inside these ranges and needn't reach their ends.
Inputs may be any that keep to these rules, and one draw needn't show every extreme that they name: `tile_block`: slot 0 of block b names entry b, the block itself. `tile_count`: some block has all 8 slots in use. `matching`: each row is a permutation of the 768 nodes.
All inputs are finite; a program needn't handle non-finite values.
Results may differ from the reference program's by a relative error of at most 0.035.
Values may be sent and summed in bfloat16 or wider, within the bound.
No kernel may reach another device: no remote copies, remote signals or barrier semaphores. Data moves between devices by JAX's collectives and lax.ppermute only.
A program may use at most 128 MiB of HBM per device.

```python
import jax
import jax.numpy as jnp
from jax import lax

D = 256
HEADS = 8
BLOCK = 128
NBLK = 6
TMAX = 8
CAP = 1
NODES = 768
HALO = 32
PARTITIONS = 256
TOTAL = 196608
N_GROUP = 8
N_DOM = 32


def key_parts(key):
    drawn_draw = jax.random.normal(key, (TOTAL, D), jnp.float32)
    return drawn_draw


def slot_counts(key):
    partitions = TOTAL // NODES
    load_limit = jax.random.randint(jax.random.fold_in(key, 41), (partitions, 1), 5, TMAX + 1)
    counts = jax.random.randint(jax.random.fold_in(key, 42), (partitions, NBLK), 5, load_limit + 1)
    return counts.at[0, 0].set(TMAX).astype(jnp.int32)


def draw_key_rows(key, part):
    drawn_draw = key_parts(key)
    return jnp.clip(drawn_draw, -6.0, 6.0).astype(jnp.bfloat16)


def draw_query_rows(key, part):
    key = jax.random.fold_in(key, 2)
    own_draw = jax.random.normal(key, (TOTAL, D), jnp.float32)
    return jnp.clip(own_draw, -6.0, 6.0).astype(jnp.bfloat16)


def draw_tile_block(key, part):
    counts = slot_counts(key)
    key = jax.random.fold_in(key, 3)
    partitions = TOTAL // NODES
    picked_rows = jax.random.randint(jax.random.fold_in(key, 5), (partitions, NBLK, TMAX), 0, NBLK + HALO)
    orders = jax.vmap(lambda one_key: jax.random.permutation(one_key, HALO))(jax.random.split(key, partitions))
    slot_index = jnp.arange(TMAX, dtype=jnp.int32)[None, None, :]
    own_index = jnp.arange(NBLK, dtype=jnp.int32)[None, :, None]
    live = (slot_index >= 1) & (slot_index < counts[:, :, None])
    live_flat = live.reshape(partitions, NBLK * TMAX).astype(jnp.int32)
    rank_flat = jnp.cumsum(live_flat, axis=1) - 1
    halo_pick = jnp.take_along_axis(orders.astype(jnp.int32), jnp.clip(rank_flat, 0, HALO - 1), axis=1)
    halo_pick = (NBLK + halo_pick).reshape(partitions, NBLK, TMAX)
    early = live & (rank_flat.reshape(partitions, NBLK, TMAX) < HALO)
    block_table = jnp.where(early, halo_pick, picked_rows)
    block_table = jnp.where(slot_index == 0, own_index, block_table)
    block_table = block_table.at[0, 0, 1].set(NBLK + HALO - 1)
    return block_table.astype(jnp.int32)


def draw_tile_count(key, part):
    counts = slot_counts(key)
    return counts


def place_ends(array, rng, smallest, top_value):
    place = [jax.random.randint(jax.random.fold_in(rng, axis), (), 0, length) for axis, length in enumerate(array.shape)]
    widest = array.shape.index(max(array.shape))
    next_to = place[:widest] + [(place[widest] + 1) % array.shape[widest]] + place[widest + 1:]
    return array.at[tuple(place)].set(smallest).at[tuple(next_to)].set(top_value)


def shard_levels(rng, shape, cuts, smallest, largest):
    loudness, own = 1.0, jax.random.fold_in(rng, 6)
    for axis_at, parts in cuts:
        steps = jnp.exp(jax.random.uniform(jax.random.fold_in(own, axis_at), (parts,), jnp.float32, smallest / len(cuts), largest / len(cuts)))
        loudness = loudness * jnp.repeat(steps, shape[axis_at] // parts).reshape([-1 if axis == axis_at else 1 for axis in range(len(shape))])
    return loudness


def gaussian(key, dims, deviation, limit, shards=(), held_as=jnp.bfloat16):
    factor_of = shard_levels(key, dims, shards, -0.22, 0.18) if shards else 1.0
    entries = jax.random.normal(key, dims, jnp.float32) * deviation * factor_of
    return jnp.minimum(jnp.maximum(entries, -limit), limit).astype(held_as)


def setup_inputs(seed: int = 0) -> dict:
    key_of = jax.random.split(jax.random.key(seed), 11)
    query_rows = draw_query_rows(jax.random.fold_in(key_of[10], 71), 0)
    key_rows = draw_key_rows(jax.random.fold_in(key_of[10], 71), 0)
    value_rows = gaussian(key_of[2], (TOTAL, D), 1.0, 6.0, ((0, 256),))
    out_weight = gaussian(key_of[3], (D, D), (D // 16) ** -0.5, 1.5)
    grad_update = gaussian(key_of[4], (TOTAL, D), 1.0, 6.0, ((0, 256),))
    expander_bias = jnp.clip(jax.random.uniform(key_of[5], (HEADS,), jnp.float32, 1.0, 5.0), 1.0, 5.0)
    tile_block = draw_tile_block(jax.random.fold_in(key_of[10], 71), 0)
    tile_count = draw_tile_count(jax.random.fold_in(key_of[10], 71), 0)
    send_block = place_ends(jax.random.randint(key_of[8], (PARTITIONS, HALO), 0, NBLK), jax.random.fold_in(key_of[8], 1), 0, NBLK - 1).astype(jnp.int32)
    matching = jax.vmap(lambda own: jax.random.permutation(own, NODES))(jax.random.split(key_of[9], PARTITIONS * 3)).reshape((PARTITIONS, 3, NODES)).astype(jnp.int32)
    return dict(query_rows=query_rows, key_rows=key_rows, value_rows=value_rows, out_weight=out_weight, grad_update=grad_update, expander_bias=expander_bias, tile_block=tile_block, tile_count=tile_count, send_block=send_block, matching=matching)


HIGH = lax.Precision.HIGHEST


def rounded(values_f):
    return lax.optimization_barrier(values_f.astype(jnp.bfloat16)).astype(jnp.float32)


def reference(query_rows, key_rows, value_rows, out_weight, grad_update, expander_bias, tile_block, tile_count, send_block, matching):
    partitions = N_GROUP * N_DOM
    head_dim = D // HEADS
    score_scale = head_dim ** -0.5
    key_blocks = key_rows.reshape(partitions, NBLK, BLOCK, D)
    value_blocks = value_rows.reshape(partitions, NBLK, BLOCK, D)
    key_nodes = key_rows.reshape(partitions, NODES, D)
    value_nodes = value_rows.reshape(partitions, NODES, D)
    query_nodes = query_rows.reshape(partitions, NODES, D)
    grad_nodes = grad_update.reshape(partitions, NODES, D)
    halo_peer = (jnp.arange(HALO) // CAP).astype(jnp.int32)
    halo_slot = (jnp.arange(HALO) % CAP).astype(jnp.int32)

    def halo_sources(partition):
        senders = (partition // N_DOM) * N_DOM + halo_peer
        return senders, (partition % N_DOM) * CAP + halo_slot

    def forward_backward(partition):
        senders, slots_at = halo_sources(partition)
        picked_blocks = send_block[senders, slots_at]
        table_keys = jnp.concatenate([key_blocks[partition], key_blocks[senders, picked_blocks]], axis=0)
        table_values = jnp.concatenate([value_blocks[partition], value_blocks[senders, picked_blocks]], axis=0)
        chosen = tile_block[partition]
        tile_keys = table_keys[chosen].astype(jnp.float32).reshape(NBLK, TMAX, BLOCK, HEADS, head_dim)
        tile_values = table_values[chosen].astype(jnp.float32).reshape(NBLK, TMAX, BLOCK, HEADS, head_dim)
        partners = [partition ^ (partitions >> (turn + 1)) for turn in range(3)]
        far_keys = jnp.stack([key_nodes[partners[turn]][matching[partition, turn]] for turn in range(3)])
        far_keys = far_keys.astype(jnp.float32).reshape(3, NODES, HEADS, head_dim)
        far_values = jnp.stack([value_nodes[partners[turn]][matching[partition, turn]] for turn in range(3)])
        far_values = far_values.astype(jnp.float32).reshape(3, NODES, HEADS, head_dim)
        queries_flat = query_nodes[partition].astype(jnp.float32).reshape(NODES, HEADS, head_dim)
        query_heads = queries_flat.reshape(NBLK, BLOCK, HEADS, head_dim)
        tiles = jnp.einsum("bqhd,btkhd->bqhtk", query_heads, tile_keys) * score_scale
        live_slots = jnp.arange(TMAX)[None, :] < tile_count[partition][:, None]
        tiles = jnp.where(live_slots[:, None, None, :, None], tiles, -jnp.inf)
        edge_scores = jnp.einsum("nhd,mnhd->nhm", queries_flat, far_keys) * score_scale + expander_bias[None, :, None]
        row_top = jnp.maximum(tiles.max(axis=(3, 4)).reshape(NODES, HEADS), edge_scores.max(axis=2))
        top_heads = row_top.reshape(NBLK, BLOCK, HEADS)
        tile_exp = jnp.exp(tiles - top_heads[..., None, None])
        edge_exp = jnp.exp(edge_scores - row_top[..., None])
        row_total = tile_exp.sum(axis=(3, 4)).reshape(NODES, HEADS) + edge_exp.sum(axis=2)
        tile_prob = tile_exp / row_total.reshape(NBLK, BLOCK, HEADS)[..., None, None]
        edge_prob = edge_exp / row_total[..., None]
        tile_weight = rounded(tile_prob)
        edge_weight = rounded(edge_prob)
        mixed = jnp.einsum("bqhtk,btkhd->bqhd", tile_weight, tile_values).reshape(NODES, HEADS, head_dim)
        mixed = mixed + jnp.einsum("nhm,mnhd->nhd", edge_weight, far_values)
        attended = mixed.reshape(NODES, D).astype(jnp.bfloat16)
        update = jnp.dot(attended, out_weight, preferred_element_type=jnp.float32).astype(jnp.bfloat16)
        grads = grad_nodes[partition]
        grad_attended = jnp.dot(grads, out_weight.T, preferred_element_type=jnp.float32).astype(jnp.bfloat16)
        weight_term = jnp.dot(attended.T, grads, preferred_element_type=jnp.float32)
        grad_flat = grad_attended.astype(jnp.float32).reshape(NODES, HEADS, head_dim)
        row_delta = jnp.sum(grad_flat * attended.astype(jnp.float32).reshape(NODES, HEADS, head_dim), axis=2)
        grad_heads = grad_flat.reshape(NBLK, BLOCK, HEADS, head_dim)
        delta_heads = row_delta.reshape(NBLK, BLOCK, HEADS)
        tile_gprob = jnp.einsum("bqhd,btkhd->bqhtk", grad_heads, tile_values)
        tile_gscore = rounded(tile_prob * (tile_gprob - delta_heads[..., None, None]) * score_scale)
        edge_gprob = jnp.einsum("nhd,mnhd->nhm", grad_flat, far_values)
        edge_gscore = rounded(edge_prob * (edge_gprob - row_delta[..., None]) * score_scale)
        query_grad = jnp.einsum("bqhtk,btkhd->bqhd", tile_gscore, tile_keys).reshape(NODES, D)
        query_grad = query_grad + jnp.einsum("nhm,mnhd->nhd", edge_gscore, far_keys).reshape(NODES, D)
        tile_kterms = jnp.einsum("bqhtk,bqhd->btkhd", tile_gscore, query_heads).reshape(NBLK, TMAX, BLOCK, D)
        tile_vterms = jnp.einsum("bqhtk,bqhd->btkhd", tile_weight, grad_heads).reshape(NBLK, TMAX, BLOCK, D)
        slot_onehot = (chosen[..., None] == jnp.arange(NBLK + HALO, dtype=jnp.int32)).astype(jnp.float32)
        table_kgrad = jnp.einsum("btu,btrc->urc", slot_onehot, tile_kterms, precision=HIGH)
        table_vgrad = jnp.einsum("btu,btrc->urc", slot_onehot, tile_vterms, precision=HIGH)
        edge_kterms = jnp.einsum("nhm,nhd->mnhd", edge_gscore, queries_flat).reshape(3, NODES, D)
        edge_vterms = jnp.einsum("nhm,nhd->mnhd", edge_weight, grad_flat).reshape(3, NODES, D)
        placed_key = jnp.stack([jnp.zeros((NODES, D), jnp.bfloat16).at[matching[partition, turn]].set(edge_kterms[turn].astype(jnp.bfloat16)) for turn in range(3)])
        placed_value = jnp.stack([jnp.zeros((NODES, D), jnp.bfloat16).at[matching[partition, turn]].set(edge_vterms[turn].astype(jnp.bfloat16)) for turn in range(3)])
        return (update, query_grad, table_kgrad[:NBLK], table_vgrad[:NBLK],
                table_kgrad[NBLK:].astype(jnp.bfloat16), table_vgrad[NBLK:].astype(jnp.bfloat16),
                placed_key, placed_value, weight_term)

    outputs = lax.map(forward_backward, jnp.arange(partitions, dtype=jnp.int32))
    updates, query_grads, own_key, own_value, halo_key, halo_value, placed_key, placed_value, weight_terms = outputs

    def collect(partition):
        senders, slots_at = halo_sources(partition)
        owner_map = (send_block[partition][:, None] == jnp.arange(NBLK, dtype=jnp.int32)).astype(jnp.float32)
        incoming_key = halo_key[senders, slots_at].astype(jnp.float32)
        incoming_value = halo_value[senders, slots_at].astype(jnp.float32)
        key_sum = own_key[partition] + jnp.einsum("sb,src->brc", owner_map, incoming_key, precision=HIGH)
        value_sum = own_value[partition] + jnp.einsum("sb,src->brc", owner_map, incoming_value, precision=HIGH)
        key_sum = key_sum.reshape(NODES, D)
        value_sum = value_sum.reshape(NODES, D)
        for turn in range(3):
            partner = partition ^ (partitions >> (turn + 1))
            key_sum = key_sum + placed_key[partner, turn].astype(jnp.float32)
            value_sum = value_sum + placed_value[partner, turn].astype(jnp.float32)
        return key_sum, value_sum

    key_grads, value_grads = lax.map(collect, jnp.arange(partitions, dtype=jnp.int32))
    weight_grad = jnp.sum(weight_terms, axis=0) * (TOTAL ** -0.5)
    return (updates.reshape(TOTAL, D), query_grads.reshape(TOTAL, D), key_grads.reshape(TOTAL, D),
            value_grads.reshape(TOTAL, D), weight_grad)
```

```python
import functools

import jax
import jax.numpy as jnp
from jax import lax
from jax.experimental import pallas as pl
from jax.experimental.pallas import tpu as pltpu
from jax.sharding import PartitionSpec as P

F32, BF16 = jnp.float32, jnp.bfloat16
LOG2E = 1.4426950408889634
GATHER, PREPARE, FORWARD, MERGE, BACKWARD, COLLECT, FINISH = (
    round(1.15e9 * us) for us in (0.5, 1, 2, 2, 14, 1, 1)
)
BUFFERS = 2
VMEM_LIMIT = 56 * 1024 * 1024
ROWS_ACROSS = (((1,), (1,)), ((), ()))
ROWS_DOWN = (((0,), (0,)), ((), ()))


def whole(shape):
    return pl.BlockSpec(shape, lambda *_: (0,) * len(shape), pipeline_mode=pl.Buffered(1))


def params():
    return pltpu.CompilerParams(vmem_limit_bytes=VMEM_LIMIT)


def cost(flops, moved):
    return pl.CostEstimate(flops=flops, bytes_accessed=moved, transcendentals=0)


def dot(a, b, dims=(((1,), (0,)), ((), ()))):
    return lax.dot_general(a, b, dims, preferred_element_type=F32)


def gather_kernel(send_block, key_ref, value_ref, sent_ref, rows, sems):
    width = key_ref.shape[1]
    block_rows = sent_ref.shape[1]
    rows[:, :width] = key_ref[...]
    rows[:, width:] = value_ref[...]
    copies = []
    for slot in range(sent_ref.shape[0]):
        start = pl.multiple_of(send_block[slot] * block_rows, block_rows)
        copy = pltpu.make_async_copy(
            rows.at[pl.ds(start, block_rows)], sent_ref.at[slot], sems.at[slot]
        )
        copy.start()
        copies.append(copy)
    for copy in copies:
        copy.wait()


def outgoing(send_block, key_rows, value_rows, block_rows):
    nodes, width = key_rows.shape
    slots = send_block.shape[0]
    return pl.pallas_call(
        gather_kernel,
        grid_spec=pltpu.PrefetchScalarGridSpec(
            num_scalar_prefetch=1,
            grid=(1,),
            in_specs=[whole((nodes, width)), whole((nodes, width))],
            out_specs=[pl.BlockSpec(memory_space=pl.ANY), whole((nodes, 2 * width))],
            scratch_shapes=[
                pltpu.SemaphoreType.DMA((slots,)),
            ],
        ),
        out_shape=[
            jax.ShapeDtypeStruct((slots, block_rows, 2 * width), BF16),
            jax.ShapeDtypeStruct((nodes, 2 * width), BF16),
        ],
        compiler_params=params(),
        cost_estimate=cost(GATHER, 1 << 10),
        name="gather_out",
    )(send_block, key_rows, value_rows)


def prepare_kernel(query_ref, grad_ref, weight_ref, match_ref, attended_ref, *placed):
    nodes, width = query_ref.shape
    grads = dot(grad_ref[...], weight_ref[...], ROWS_ACROSS).astype(BF16)
    attended_ref[...] = grads
    both = jnp.concatenate([query_ref[...], grads], axis=1)
    target = lax.broadcasted_iota(jnp.int32, (nodes, nodes), 0)
    for turn, placed_ref in enumerate(placed):
        chosen = (target == match_ref[turn : turn + 1, :]).astype(F32).astype(BF16)
        placed_ref[...] = dot(chosen, both).astype(BF16)


def prepare(query_rows, grad_update, out_weight, matching):
    nodes, width = query_rows.shape
    turns = matching.shape[0]
    return pl.pallas_call(
        prepare_kernel,
        grid=(1,),
        in_specs=[
            whole((nodes, width)),
            whole((nodes, width)),
            whole((width, width)),
            whole((turns, nodes)),
        ],
        out_specs=[whole((nodes, width))] + [whole((nodes, 2 * width))] * turns,
        out_shape=[jax.ShapeDtypeStruct((nodes, width), BF16)]
        + [jax.ShapeDtypeStruct((nodes, 2 * width), BF16)] * turns,
        compiler_params=params(),
        cost_estimate=cost(1150 * 10**6, 1 << 10),
        name="prepare",
    )(query_rows, grad_update, out_weight, matching)


def head_rows(lanes, heads, per):
    return jnp.concatenate([lanes[:, h * per : (h + 1) * per] for h in range(heads)], axis=0)


def head_lanes(stacked, heads, dim):
    return jnp.concatenate(
        [
            jnp.sum(stacked[h * dim : (h + 1) * dim], axis=0, keepdims=True)
            for h in range(heads)
        ],
        axis=1,
    )


def spread(lanes, heads, dim, per):
    return jnp.concatenate(
        [
            jnp.broadcast_to(lanes[:, h * per : (h + 1) * per], (dim, per))
            for h in range(heads)
        ],
        axis=0,
    )


def diagonal(product, heads, dim, per):
    return jnp.concatenate(
        [
            product[h * dim : (h + 1) * dim, h * per : (h + 1) * per]
            for h in range(heads)
        ],
        axis=0,
    )


def masked_heads(rows, heads, dim):
    lane = lax.broadcasted_iota(jnp.int32, rows.shape, 1) // dim
    wide = rows.astype(F32)
    return jnp.concatenate(
        [jnp.where(lane == h, wide, 0.0) for h in range(heads)], axis=0
    ).astype(BF16)


def fill_table(table, key_ref, value_ref, halo_ref, sem):
    blocks = table.shape[0] - halo_ref.shape[0]
    per, width = table.shape[1], key_ref.shape[1]
    copy = pltpu.make_async_copy(halo_ref, table.at[pl.ds(blocks, halo_ref.shape[0])], sem)
    copy.start()
    for block in range(blocks):
        table[block, :, :width] = key_ref[block * per : (block + 1) * per, :]
        table[block, :, width:] = value_ref[block * per : (block + 1) * per, :]
    return copy


def live(values, start, rows):
    if start + values.shape[0] <= 5 * values.shape[1] // 4:
        return values
    row = lax.broadcasted_iota(jnp.int32, values.shape, 0) + start
    return jnp.where(row < rows, values, -jnp.inf)


def forward_kernel(
    heads, dim, tile_block, tile_count, key_ref, value_ref, halo_ref, query_ref,
    stats_out, mixed_out, table, picked, scores, raised, sem,
):
    blocks, slots = tile_count.shape[0], tile_block.shape[0] // tile_count.shape[0]
    nodes, features = query_ref.shape
    per = nodes // blocks
    width = heads * dim
    scale2 = dim**-0.5 * LOG2E
    span = slots // 2 * per
    parts = [slice(0, span), slice(span, 2 * span)]
    fill_table(table, key_ref, value_ref, halo_ref, sem).wait()

    def block_step(step, _):
        buffer = 0
        at = pl.ds(pl.multiple_of(step * per, per), per)
        for slot in range(slots):
            picked[buffer, slot * per : (slot + 1) * per, :] = table[tile_block[step * slots + slot]]
        live_rows = tile_count[step] * per
        for half in range(2):
            unit = step * 2 + half
            place = half
            keys = slice(half * width, (half + 1) * width)
            values = slice(features + half * width, features + (half + 1) * width)
            query_masked = masked_heads(query_ref[at, keys], heads, dim)
            top = None
            for part in parts:
                block = dot(picked[buffer, part, keys], query_masked, ROWS_ACROSS)
                block = live(block, part.start, live_rows)
                scores[place, part, :] = block
                part_top = jnp.max(block.reshape(span // 8, 8, heads * per), axis=0)
                top = part_top if top is None else jnp.maximum(top, part_top)
            top = jnp.max(top, axis=0, keepdims=True) * scale2
            total = jnp.zeros((8, heads * per), F32)
            for part in parts:
                block = jnp.exp2(scores[place, part, :] * scale2 - top)
                raised[place, part, :] = block.astype(BF16)
                total = total + jnp.sum(block.reshape(span // 8, 8, heads * per), axis=0)
            total = jnp.sum(total, axis=0, keepdims=True)
            mixed = dot(picked[buffer, :, values], raised[place], ROWS_DOWN)
            mixed_out[unit] = diagonal(mixed, heads, dim, per)
            stats_out[unit] = jnp.concatenate(
                [top, total, jnp.zeros((6, heads * per), F32)], axis=0
            )
        return 0

    lax.fori_loop(0, blocks, block_step, 0)


def merge_kernel(
    heads, dim, bias_ref, group_ref, below_1, above_1, below_2, above_2, below_4, above_4, match_ref,
    query_ref, grad_ref, update_grad_ref, out_weight, stats_ref, mixed_ref,
    update_out, weight_out, stats_out, query_grad_out, edge_out, weight_sum, far, sems,
):
    units = stats_ref.shape[0]
    blocks = units // 2
    nodes, features = query_ref.shape
    per = nodes // blocks
    width = heads * dim
    scale = dim**-0.5
    scale2 = scale * LOG2E
    lane_node = lax.broadcasted_iota(jnp.int32, (per, nodes), 1)
    place = group_ref[0]
    half_rows = nodes // 2

    def bring(turn, distance, below, above):
        below_is_partner = lax.rem(place // distance, 2) == 1

        @pl.when(below_is_partner)
        def _():
            pltpu.make_async_copy(below, far.at[turn], sems.at[turn]).start()

        @pl.when(jnp.logical_not(below_is_partner))
        def _():
            pltpu.make_async_copy(above, far.at[turn], sems.at[turn]).start()

    bring(2, 1, below_1, above_1)
    bring(1, 2, below_2, above_2)
    upper = pltpu.make_async_copy(below_4, far.at[0, pl.ds(0, half_rows)], sems.at[0])
    lower = pltpu.make_async_copy(above_4, far.at[0, pl.ds(half_rows, half_rows)], sems.at[3])
    upper.start()
    lower.start()
    weight_sum[...] = jnp.zeros_like(weight_sum)
    edge_out[...] = jnp.zeros_like(edge_out)
    for turn in (1, 2):
        pltpu.make_async_copy(below_1, far.at[turn], sems.at[turn]).wait()
    upper.wait()
    lower.wait()

    def block_step(step, _):
        at = pl.ds(pl.multiple_of(step * per, per), per)
        query_t = query_ref[at, :].astype(F32).T
        grad_t = grad_ref[at, :].astype(F32).T
        chosen, far_keys, far_values = [], [], []
        for turn in range(3):
            pick = (lane_node == match_ref[at, turn : turn + 1]).astype(F32).astype(BF16)
            chosen.append(pick)
            found = dot(pick, far[turn])
            far_keys.append(found[:, :features].T)
            far_values.append(found[:, features:].T)
        attended_t = []
        rows = [[], [], []]
        for half in range(2):
            unit = step * 2 + half
            of = slice(half * width, (half + 1) * width)
            bias = jnp.concatenate(
                [jnp.full((1, per), bias_ref[half * heads + h] * LOG2E, F32) for h in range(heads)],
                axis=1,
            )
            scores = [
                head_lanes(query_t[of] * far_keys[turn][of], heads, dim) * scale2 + bias
                for turn in range(3)
            ]
            tile_top, tile_total = stats_ref[unit, 0:1, :], stats_ref[unit, 1:2, :]
            top = jnp.maximum(jnp.maximum(tile_top, scores[0]), jnp.maximum(scores[1], scores[2]))
            shrink = jnp.exp2(tile_top - top)
            raised = [jnp.exp2(scores[turn] - top) for turn in range(3)]
            total = tile_total * shrink + (raised[0] + raised[1] + raised[2])
            inverse = 1.0 / total
            probs = [raised[turn] * inverse for turn in range(3)]
            weights = [probs[turn].astype(BF16).astype(F32) for turn in range(3)]
            mixed = mixed_ref[unit] * spread(shrink * inverse, heads, dim, per)
            for turn in range(3):
                mixed = mixed + spread(weights[turn], heads, dim, per) * far_values[turn][of]
            attended = mixed.astype(BF16)
            attended_t.append(attended)
            delta = head_lanes(grad_t[of] * attended.astype(F32), heads, dim)
            stats_out[unit] = jnp.concatenate(
                [top + jnp.log2(total), delta, jnp.zeros((6, heads * per), F32)], axis=0
            )
            query_grad = jnp.zeros((width, per), F32)
            for turn in range(3):
                grad_prob = head_lanes(grad_t[of] * far_values[turn][of], heads, dim)
                dscore = (probs[turn] * (grad_prob - delta) * scale).astype(BF16).astype(F32)
                query_grad = query_grad + spread(dscore, heads, dim, per) * far_keys[turn][of]
                rows[turn] += [head_rows(dscore, heads, per), head_rows(weights[turn], heads, per)]
            query_grad_out[unit] = query_grad
        both = jnp.concatenate(attended_t, axis=0)
        update_out[at, :] = dot(both, out_weight[...], ROWS_DOWN).astype(BF16)
        product = dot(both, update_grad_ref[at, :])
        weight_sum[...] += product
        for turn in range(3):
            edge_out[turn] += dot(jnp.concatenate(rows[turn], axis=0).astype(BF16), chosen[turn])
        return 0

    lax.fori_loop(0, blocks, block_step, 0)
    for piece in range(weight_out.shape[0]):
        rows_each = weight_out.shape[1]
        weight_out[piece] = weight_sum[piece * rows_each : (piece + 1) * rows_each, :].astype(BF16)


def backward_kernel(
    heads, dim, tile_block, tile_count, key_ref, value_ref, halo_ref, query_ref, grad_ref,
    stats_ref, edge_ref, returned_ref, own_terms_ref, query_out,
    table, picked, weights, dscores, terms, sem,
):
    blocks, slots = tile_count.shape[0], tile_block.shape[0] // tile_count.shape[0]
    nodes, features = query_ref.shape
    per = nodes // blocks
    width = heads * dim
    scale = dim**-0.5
    scale2 = scale * LOG2E
    span = slots // 2 * per
    parts = [slice(0, span), slice(span, 2 * span)]
    halo_copy = fill_table(table, key_ref, value_ref, halo_ref, sem)
    terms[...] = jnp.zeros_like(terms)
    returned_ref[:, per:, :] = jnp.zeros_like(returned_ref[:, per:, :])
    halo_copy.wait()

    def block_step(step, _):
        buffer = 0
        at = pl.ds(pl.multiple_of(step * per, per), per)
        entries = [tile_block[step * slots + slot] for slot in range(slots)]
        for slot in range(slots):
            picked[buffer, slot * per : (slot + 1) * per, :] = table[entries[slot]]
        live_rows = tile_count[step] * per
        for half in range(2):
            unit = step * 2 + half
            place = half
            keys = slice(half * width, (half + 1) * width)
            values = slice(features + half * width, features + (half + 1) * width)
            query_masked = masked_heads(query_ref[at, keys], heads, dim)
            grad_masked = masked_heads(grad_ref[at, keys], heads, dim)
            log_total, delta = stats_ref[unit, 0:1, :], stats_ref[unit, 1:2, :]
            for part in parts:
                block = dot(picked[buffer, part, keys], query_masked, ROWS_ACROSS)
                block = live(block, part.start, live_rows)
                prob = jnp.exp2(block * scale2 - log_total)
                weights[place, part, :] = prob.astype(BF16)
                grad_prob = dot(picked[buffer, part, values], grad_masked, ROWS_ACROSS)
                dscores[place, part, :] = (prob * scale * (grad_prob - delta)).astype(BF16)
            query_grad = dot(picked[buffer, :, keys], dscores[place], ROWS_DOWN)
            query_grad = diagonal(query_grad, heads, dim, per) + edge_ref[unit]
            query_out[at, keys] = query_grad.T
            key_terms = dot(dscores[place], query_masked)
            value_terms = dot(weights[place], grad_masked)
            for slot in range(slots):
                rows = slice(slot * per, (slot + 1) * per)
                terms[entries[slot], :, keys] += key_terms[rows]
                terms[entries[slot], :, values] += value_terms[rows]
        return 0

    lax.fori_loop(0, blocks, block_step, 0)
    own_terms_ref[...] = terms[:blocks]
    returned_ref[:, :per, :] = terms[blocks:].astype(BF16)


def run(kernel, scalars, ins, outs, scratch, estimate, name):
    specs = [whole(array.shape) if spec is None else spec for array, spec in ins]
    return pl.pallas_call(
        kernel,
        grid_spec=pltpu.PrefetchScalarGridSpec(
            num_scalar_prefetch=len(scalars),
            grid=(1,),
            in_specs=specs,
            out_specs=[whole(shape) for shape, _ in outs],
            scratch_shapes=scratch,
        ),
        out_shape=[jax.ShapeDtypeStruct(shape, dtype) for shape, dtype in outs],
        compiler_params=params(),
        cost_estimate=cost(estimate, 1 << 10),
        name=name,
    )(*scalars, *(array for array, _ in ins))


ANYWHERE = pl.BlockSpec(memory_space=pl.ANY)


def forward(scalars, key_rows, value_rows, halo, query_rows, heads):
    tile_block, tile_count = scalars
    nodes, features = query_rows.shape
    blocks, slots = tile_count.shape[0], tile_block.shape[0] // tile_count.shape[0]
    per, width = nodes // blocks, features // 2
    columns = heads // 2 * per
    return run(
        functools.partial(forward_kernel, heads // 2, features // heads),
        scalars,
        [(key_rows, None), (value_rows, None), (halo, ANYWHERE), (query_rows, None)],
        [((2 * blocks, 8, columns), F32), ((2 * blocks, width, per), F32)],
        [
            pltpu.VMEM((blocks + halo.shape[0], per, 2 * features), BF16),
            pltpu.VMEM((1, slots * per, 2 * features), BF16),
            pltpu.VMEM((BUFFERS, slots * per, columns), F32),
            pltpu.VMEM((BUFFERS, slots * per, columns), BF16),
            pltpu.SemaphoreType.DMA,
        ],
        FORWARD,
        "forward",
    )


def merge(bias, group, far, match_columns, query_rows, attended_grad, grad_update, out_weight, stats, mixed):
    nodes, features = query_rows.shape
    heads = bias.shape[0]
    arrays = [match_columns, query_rows, attended_grad, grad_update, out_weight, stats, mixed]
    return run(
        functools.partial(merge_kernel, heads // 2, features // heads),
        (bias, group),
        [(array, ANYWHERE) for array in far] + [(array, None) for array in arrays],
        [
            ((nodes, features), BF16),
            ((8, features // 8, features), BF16),
            (stats.shape, F32),
            (mixed.shape, F32),
            ((3, 2 * heads, nodes), F32),
        ],
        [
            pltpu.VMEM((features, features), F32),
            pltpu.VMEM((3, nodes, 2 * features), BF16),
            pltpu.SemaphoreType.DMA((4,)),
        ],
        MERGE,
        "merge",
    )


def backward(scalars, key_rows, value_rows, halo, query_rows, attended_grad, stats, edge_part, spare, heads):
    tile_block, tile_count = scalars
    nodes, features = query_rows.shape
    blocks, slots = tile_count.shape[0], tile_block.shape[0] // tile_count.shape[0]
    per = nodes // blocks
    columns = heads // 2 * per
    count = halo.shape[0]
    return run(
        functools.partial(backward_kernel, heads // 2, features // heads),
        scalars,
        [(key_rows, None), (value_rows, None), (halo, ANYWHERE), (query_rows, None)]
        + [(attended_grad, None), (stats, None), (edge_part, None)],
        [
            ((count, per + spare, 2 * features), BF16),
            ((blocks, per, 2 * features), F32),
            ((nodes, features), F32),
        ],
        [
            pltpu.VMEM((blocks + count, per, 2 * features), BF16),
            pltpu.VMEM((1, slots * per, 2 * features), BF16),
            pltpu.VMEM((BUFFERS, slots * per, columns), BF16),
            pltpu.VMEM((BUFFERS, slots * per, columns), BF16),
            pltpu.VMEM((blocks + count, per, 2 * features), F32),
            pltpu.SemaphoreType.DMA,
        ],
        BACKWARD,
        "backward",
    )


def collect_kernel(heads, own_ref, *refs):
    placed, edges = refs[:3], refs[3:6]
    key_ref, value_ref = refs[6:]
    blocks, per, both = own_ref.shape
    two = both // 2
    width = two // 2
    dim = width // heads
    for block in range(blocks):
        key_ref[block * per : (block + 1) * per, :] = own_ref[block, :, :two]
        value_ref[block * per : (block + 1) * per, :] = own_ref[block, :, two:]
    row = lax.broadcasted_iota(jnp.int32, (4 * heads, two), 0)
    lane = lax.broadcasted_iota(jnp.int32, (4 * heads, two), 1)
    key_row = (lane // width) * (2 * heads) + lax.rem(lane, width) // dim
    key_spread = (row == key_row).astype(F32).astype(BF16)
    value_spread = (row == key_row + heads).astype(F32).astype(BF16)
    for turn in range(3):
        scalars = edges[turn][...].astype(BF16)
        dscore = dot(scalars, key_spread, ROWS_DOWN)
        weight = dot(scalars, value_spread, ROWS_DOWN)
        key_term = dscore * placed[turn][:, :two].astype(F32)
        value_term = weight * placed[turn][:, two:].astype(F32)
        key_ref[...] += key_term.astype(BF16).astype(F32)
        value_ref[...] += value_term.astype(BF16).astype(F32)


def collect(own, placed, edges, heads):
    blocks, per, both = own.shape
    out = ((blocks * per, both // 2), F32)
    arrays = [own, *placed, *edges]
    return run(
        functools.partial(collect_kernel, heads // 2),
        (),
        [(array, None) for array in arrays],
        [out, out],
        [],
        COLLECT,
        "collect",
    )


def finish_kernel(send_block, home_ref, key_in, value_in, key_ref, value_ref):
    slots, _, both = home_ref.shape
    two = both // 2
    per = home_ref.shape[1]
    key_ref[...] = key_in[...]
    value_ref[...] = value_in[...]
    for slot in range(slots):
        start = pl.multiple_of(send_block[slot] * per, per)
        key_ref[pl.ds(start, per), :] += home_ref[slot, :, :two].astype(F32)
        value_ref[pl.ds(start, per), :] += home_ref[slot, :, two:].astype(F32)


def finish(send_block, home, key_sum, value_sum, per):
    slots, _, both = home.shape
    out = (key_sum.shape, F32)
    part = pl.BlockSpec((slots, per, both), lambda *_: (0, 0, 0), pipeline_mode=pl.Buffered(1))
    return run(
        finish_kernel,
        (send_block,),
        [(home, part), (key_sum, None), (value_sum, None)],
        [out, out],
        [],
        FINISH,
        "finish",
    )


def from_partner(array, apart):
    axes = ("group", "dom")
    return lax.ppermute(array, axes, [(i, i ^ 1 << apart) for i in range(lax.axis_size(axes))])


def ahead(array, steps):
    count = lax.axis_size("group")
    return lax.ppermute(array, "group", [(i, (i + steps) % count) for i in range(count)])


def exchange(array, axis):
    return lax.all_to_all(array, axis, split_axis=0, concat_axis=0, tiled=True)


def shards(
    query_rows,
    key_rows,
    value_rows,
    out_weight,
    grad_update,
    expander_bias,
    tile_block,
    tile_count,
    send_block,
    matching,
):
    nodes, features = query_rows.shape
    heads = expander_bias.shape[0]
    tile_block = tile_block[0]
    tile_count = tile_count[0]
    send_block = send_block[0]
    matching = matching[0]
    per = nodes // tile_block.shape[0]
    devices = lax.axis_size(("group", "dom"))
    top_bit = devices.bit_length() - 1
    groups = lax.axis_size("group")

    sent, own_rows = outgoing(send_block, key_rows, value_rows, per)
    halo = exchange(sent, "dom")
    below_1, above_1 = ahead(own_rows, 1), ahead(own_rows, -1)
    attended_grad, *placed = prepare(query_rows, grad_update, out_weight, matching)
    below_1, above_1, attended_grad = lax.optimization_barrier((below_1, above_1, attended_grad))
    below_2, above_2 = ahead(below_1, 1), ahead(above_1, -1)
    below_4 = ahead(ahead(below_2[: nodes // 2], 1), 1)
    above_4 = ahead(ahead(above_2[nodes // 2 :], -1), -1)
    far = [below_1, above_1, below_2, above_2, below_4, above_4]
    group = lax.axis_index("group").astype(jnp.int32).reshape(1)
    placed = [from_partner(placed[turn], top_bit - 1 - turn) for turn in range(3)]

    scalars = (tile_block.reshape(-1), tile_count)
    stats, mixed = forward(scalars, key_rows, value_rows, halo, query_rows, heads)
    update, pieces, stats, edge_part, edges = merge(
        expander_bias, group, far, matching.T, query_rows, attended_grad, grad_update, out_weight, stats, mixed
    )
    edges = [from_partner(edges[turn], top_bit - 1 - turn) for turn in range(3)]
    pieces = exchange(pieces, "group")
    spare = features // 8 // 2
    back, own, query_grad = backward(
        scalars, key_rows, value_rows, halo, query_rows, attended_grad, stats, edge_part, spare, heads
    )
    part = pieces.astype(F32).sum(axis=0).astype(BF16)
    part = jnp.concatenate([part[:spare], part[spare:]], axis=1)
    back = back.at[:, per:, :].set(part[None])
    back, placed[1], placed[2] = lax.optimization_barrier((back, placed[1], placed[2]))
    home = exchange(back, "dom")
    key_sum, value_sum = collect(own, placed, edges, heads)
    home, key_sum, value_sum = lax.optimization_barrier((home, key_sum, value_sum))
    key_grad, value_grad = finish(send_block, home, key_sum, value_sum, per)

    summed = home[:, per:, :].astype(F32).sum(axis=0) * (nodes * devices) ** (-0.5)
    summed = jnp.concatenate([summed[:, :features], summed[:, features:]], axis=0)
    copies = jnp.broadcast_to(summed[None], (groups,) + summed.shape)
    weight_grad = exchange(copies, "group").reshape(features, features)
    return (update, query_grad, key_grad, value_grad, weight_grad)


def solution(mesh):
    rows = P(("group", "dom"), None)
    in_specs = (
        rows,
        rows,
        rows,
        P(),
        rows,
        P(),
        P(("group", "dom"), None, None),
        rows,
        rows,
        P(("group", "dom"), None, None),
    )
    out_specs = (rows, rows, rows, rows, P())
    return jax.shard_map(shards, mesh=mesh, in_specs=in_specs, out_specs=out_specs, check_vma=False)
```

```python
import functools

import jax
import jax.numpy as jnp
from jax import lax
from jax.experimental import pallas as pl
from jax.experimental.pallas import tpu as pltpu
from jax.sharding import PartitionSpec as P

F32, BF16 = jnp.float32, jnp.bfloat16
LOG2E = 1.4426950408889634
GATHER, PREPARE, FETCH, FORWARD, BACKWARD, PLACE, COLLECT, FINISH = (
    round(1.15e9 * us) for us in (0.5, 1, 1, 3, 20, 1, 1, 1)
)
BUFFERS = 2
ROWS_ACROSS = (((1,), (1,)), ((), ()))
ROWS_DOWN = (((0,), (0,)), ((), ()))


def whole(shape):
    return pl.BlockSpec(shape, lambda *_: (0,) * len(shape), pipeline_mode=pl.Buffered(1))


ANYWHERE = pl.BlockSpec(memory_space=pl.ANY)


def params(mebibytes=60):
    return pltpu.CompilerParams(vmem_limit_bytes=mebibytes << 20)


def cost(flops, moved):
    return pl.CostEstimate(flops=flops, bytes_accessed=moved, transcendentals=0)


def dot(a, b, dims=(((1,), (0,)), ((), ()))):
    return lax.dot_general(a, b, dims, preferred_element_type=F32)


def gather_kernel(send_block, key_ref, value_ref, sent_ref, rows, sems):
    width = key_ref.shape[1]
    block_rows = sent_ref.shape[1]
    rows[:, :width] = key_ref[...]
    rows[:, width:] = value_ref[...]
    copies = []
    for slot in range(sent_ref.shape[0]):
        start = pl.multiple_of(send_block[slot] * block_rows, block_rows)
        copy = pltpu.make_async_copy(
            rows.at[pl.ds(start, block_rows)], sent_ref.at[slot], sems.at[slot]
        )
        copy.start()
        copies.append(copy)
    for copy in copies:
        copy.wait()


def outgoing(send_block, key_rows, value_rows, block_rows):
    nodes, width = key_rows.shape
    slots = send_block.shape[0]
    return pl.pallas_call(
        gather_kernel,
        grid_spec=pltpu.PrefetchScalarGridSpec(
            num_scalar_prefetch=1,
            grid=(1,),
            in_specs=[whole((nodes, width)), whole((nodes, width))],
            out_specs=pl.BlockSpec(memory_space=pl.ANY),
            scratch_shapes=[
                pltpu.VMEM((nodes, 2 * width), BF16),
                pltpu.SemaphoreType.DMA((slots,)),
            ],
        ),
        out_shape=jax.ShapeDtypeStruct((slots, block_rows, 2 * width), BF16),
        compiler_params=params(),
        cost_estimate=cost(GATHER, 1 << 10),
        name="gather_out",
    )(send_block, key_rows, value_rows)


def prepare_kernel(query_ref, grad_ref, weight_ref, match_ref, attended_ref, *placed):
    nodes, width = query_ref.shape
    grads = dot(grad_ref[...], weight_ref[...], ROWS_ACROSS).astype(BF16)
    attended_ref[...] = grads
    both = jnp.concatenate([query_ref[...], grads], axis=1)
    target = lax.broadcasted_iota(jnp.int32, (nodes, nodes), 0)
    for turn, placed_ref in enumerate(placed):
        chosen = (target == match_ref[turn : turn + 1, :]).astype(F32).astype(BF16)
        placed_ref[...] = dot(chosen, both).astype(BF16)


def prepare(query_rows, grad_update, out_weight, matching):
    nodes, width = query_rows.shape
    turns = matching.shape[0]
    return pl.pallas_call(
        prepare_kernel,
        grid=(1,),
        in_specs=[
            whole((nodes, width)),
            whole((nodes, width)),
            whole((width, width)),
            whole((turns, nodes)),
        ],
        out_specs=[whole((nodes, width))] + [whole((nodes, 2 * width))] * turns,
        out_shape=[jax.ShapeDtypeStruct((nodes, width), BF16)]
        + [jax.ShapeDtypeStruct((nodes, 2 * width), BF16)] * turns,
        compiler_params=params(),
        cost_estimate=cost(1150 * 10**6, 1 << 10),
        name="prepare",
    )(query_rows, grad_update, out_weight, matching)


def head_rows(lanes, heads, per):
    return jnp.concatenate([lanes[:, h * per : (h + 1) * per] for h in range(heads)], axis=0)


def head_lanes(stacked, heads, dim):
    return jnp.concatenate(
        [
            jnp.sum(stacked[h * dim : (h + 1) * dim], axis=0, keepdims=True)
            for h in range(heads)
        ],
        axis=1,
    )


def spread(lanes, heads, dim, per):
    return jnp.concatenate(
        [
            jnp.broadcast_to(lanes[:, h * per : (h + 1) * per], (dim, per))
            for h in range(heads)
        ],
        axis=0,
    )


def diagonal(product, heads, dim, per):
    return jnp.concatenate(
        [
            product[h * dim : (h + 1) * dim, h * per : (h + 1) * per]
            for h in range(heads)
        ],
        axis=0,
    )


def masked_heads(rows, heads, dim):
    lane = lax.broadcasted_iota(jnp.int32, rows.shape, 1) // dim
    wide = rows.astype(F32)
    return jnp.concatenate(
        [jnp.where(lane == h, wide, 0.0) for h in range(heads)], axis=0
    ).astype(BF16)


def fill_table(table, key_ref, value_ref, halo_ref, sems):
    blocks = table.shape[0] - halo_ref.shape[0]
    per, width = table.shape[1], key_ref.shape[1]
    copies = [
        pltpu.make_async_copy(halo_ref, table.at[pl.ds(blocks, halo_ref.shape[0])], sems.at[2 * blocks])
    ]
    for block in range(blocks):
        for which, ref in enumerate((key_ref, value_ref)):
            source = ref.at[pl.ds(block * per, per)]
            target = table.at[block, :, pl.ds(which * width, width)]
            copies.append(pltpu.make_async_copy(source, target, sems.at[2 * block + which]))
    for copy in copies:
        copy.start()
    return copies


def live(values, start, rows):
    if start + values.shape[0] <= 5 * values.shape[1] // 4:
        return values
    row = lax.broadcasted_iota(jnp.int32, values.shape, 0) + start
    return jnp.where(row < rows, values, -jnp.inf)


def bring_halves(k_below, k_above, v_below, v_above, rows, sems):
    half, features = k_below.shape
    copies = []
    for which, pair in enumerate(((k_below, k_above), (v_below, v_above))):
        for end, ref in enumerate(pair):
            target = rows.at[pl.ds(end * half, half), pl.ds(which * features, features)]
            copies.append(pltpu.make_async_copy(ref, target, sems.at[2 * end + which]))
    for copy in copies:
        copy.start()
    return copies


def forward_kernel(
    heads, dim, tile_block, tile_count, bias_ref, halo_ref, key_ref, value_ref,
    k_below, k_above, v_below, v_above, match_ref, far_1, far_2, query_ref, grad_ref, update_grad_ref,
    out_weight, update_out, weight_out, stats_out, query_grad_out, edge_out,
    table, picked, scores, raised, weight_sum, rows_4, far_0, sem, sems,
):
    blocks, slots = tile_count.shape[0], tile_block.shape[0] // tile_count.shape[0]
    nodes, features = query_ref.shape
    per = nodes // blocks
    width = heads * dim
    scale = dim**-0.5
    scale2 = scale * LOG2E
    span = slots // 2 * per
    parts = [slice(0, span), slice(span, 2 * span)]
    far = (far_0, far_1, far_2)
    first = bring_halves(k_below, k_above, v_below, v_above, rows_4, sems)
    copies = fill_table(table, key_ref, value_ref, halo_ref, sem)
    target_node = lax.broadcasted_iota(jnp.int32, (nodes, nodes), 0)
    chosen = (target_node == match_ref[...]).astype(F32).astype(BF16)
    for copy in first:
        copy.wait()
    far_0[...] = dot(rows_4[...], chosen, ROWS_DOWN).astype(BF16)
    weight_sum[...] = jnp.zeros_like(weight_sum)
    for copy in copies:
        copy.wait()

    def block_step(step, _):
        buffer = 0
        at = pl.ds(pl.multiple_of(step * per, per), per)
        for slot in range(slots):
            picked[buffer, slot * per : (slot + 1) * per, :] = table[tile_block[step * slots + slot]]
        live_rows = tile_count[step] * per
        query_t = query_ref[at, :].astype(F32).T
        grad_t = grad_ref[at, :].astype(F32).T
        far_keys = [far[turn][:features, at].astype(F32) for turn in range(3)]
        far_values = [far[turn][features:, at].astype(F32) for turn in range(3)]
        attended_t = []
        rows = [[], [], []]
        for half in range(2):
            unit = step * 2 + half
            of = slice(half * width, (half + 1) * width)
            values = slice(features + half * width, features + (half + 1) * width)
            bias = jnp.concatenate(
                [jnp.full((1, per), bias_ref[half * heads + h] * LOG2E, F32) for h in range(heads)],
                axis=1,
            )
            edge_scores = [
                head_lanes(query_t[of] * far_keys[turn][of], heads, dim) * scale2 + bias
                for turn in range(3)
            ]
            query_masked = masked_heads(query_ref[at, of], heads, dim)
            top = None
            for part in parts:
                block = dot(picked[buffer, part, of], query_masked, ROWS_ACROSS)
                block = live(block, part.start, live_rows)
                scores[half, part, :] = block
                part_top = jnp.max(block.reshape(span // 8, 8, heads * per), axis=0)
                top = part_top if top is None else jnp.maximum(top, part_top)
            top = jnp.max(top, axis=0, keepdims=True) * scale2
            for turn in range(3):
                top = jnp.maximum(top, edge_scores[turn])
            total = jnp.zeros((8, heads * per), F32)
            for part in parts:
                block = jnp.exp2(scores[half, part, :] * scale2 - top)
                raised[half, part, :] = block.astype(BF16)
                total = total + jnp.sum(block.reshape(span // 8, 8, heads * per), axis=0)
            total = jnp.sum(total, axis=0, keepdims=True)
            edge_raised = [jnp.exp2(edge_scores[turn] - top) for turn in range(3)]
            total = total + (edge_raised[0] + edge_raised[1] + edge_raised[2])
            inverse = 1.0 / total
            probs = [edge_raised[turn] * inverse for turn in range(3)]
            weights = [probs[turn].astype(BF16).astype(F32) for turn in range(3)]
            mixed = dot(picked[buffer, :, values], raised[half], ROWS_DOWN)
            mixed = diagonal(mixed, heads, dim, per) * spread(inverse, heads, dim, per)
            for turn in range(3):
                mixed = mixed + spread(weights[turn], heads, dim, per) * far_values[turn][of]
            attended = mixed.astype(BF16)
            attended_t.append(attended)
            delta = head_lanes(grad_t[of] * attended.astype(F32), heads, dim)
            stats_out[unit] = jnp.concatenate(
                [top + jnp.log2(total), delta, jnp.zeros((6, heads * per), F32)], axis=0
            )
            query_grad = jnp.zeros((width, per), F32)
            for turn in range(3):
                grad_prob = head_lanes(grad_t[of] * far_values[turn][of], heads, dim)
                dscore = (probs[turn] * (grad_prob - delta) * scale).astype(BF16).astype(F32)
                query_grad = query_grad + spread(dscore, heads, dim, per) * far_keys[turn][of]
                rows[turn] += [head_rows(dscore, heads, per), head_rows(weights[turn], heads, per)]
            query_grad_out[unit] = query_grad
        both = jnp.concatenate(attended_t, axis=0)
        update_out[at, :] = dot(both, out_weight[...], ROWS_DOWN).astype(BF16)
        weight_sum[...] += dot(both, update_grad_ref[at, :])
        for turn in range(3):
            edge_out[turn, :, at] = jnp.concatenate(rows[turn], axis=0)
        return 0

    lax.fori_loop(0, blocks, block_step, 0)
    for piece in range(weight_out.shape[0]):
        rows_each = weight_out.shape[1]
        weight_out[piece] = weight_sum[piece * rows_each : (piece + 1) * rows_each, :].astype(BF16)


def backward_kernel(
    heads, dim, tile_block, tile_count, key_ref, value_ref, halo_ref, query_ref, grad_ref,
    stats_ref, edge_ref, returned_ref, own_terms_ref, query_out,
    table, picked, weights, dscores, terms, packed, sem, out_sems,
):
    blocks, slots = tile_count.shape[0], tile_block.shape[0] // tile_count.shape[0]
    nodes, features = query_ref.shape
    per = nodes // blocks
    width = heads * dim
    scale = dim**-0.5
    scale2 = scale * LOG2E
    span = slots // 2 * per
    parts = [slice(0, span), slice(span, 2 * span)]
    copies = fill_table(table, key_ref, value_ref, halo_ref, sem)
    terms[...] = jnp.zeros_like(terms)
    for copy in copies:
        copy.wait()

    def block_step(step, _):
        buffer = 0
        at = pl.ds(pl.multiple_of(step * per, per), per)
        entries = [tile_block[step * slots + slot] for slot in range(slots)]
        for slot in range(slots):
            picked[buffer, slot * per : (slot + 1) * per, :] = table[entries[slot]]
        live_rows = tile_count[step] * per
        for half in range(2):
            unit = step * 2 + half
            place = half
            keys = slice(half * width, (half + 1) * width)
            values = slice(features + half * width, features + (half + 1) * width)
            query_masked = masked_heads(query_ref[at, keys], heads, dim)
            grad_masked = masked_heads(grad_ref[at, keys], heads, dim)
            log_total, delta = stats_ref[unit, 0:1, :], stats_ref[unit, 1:2, :]
            for part in parts:
                block = dot(picked[buffer, part, keys], query_masked, ROWS_ACROSS)
                block = live(block, part.start, live_rows)
                prob = jnp.exp2(block * scale2 - log_total)
                weights[place, part, :] = prob.astype(BF16)
                grad_prob = dot(picked[buffer, part, values], grad_masked, ROWS_ACROSS)
                dscores[place, part, :] = (prob * scale * (grad_prob - delta)).astype(BF16)
            query_grad = dot(picked[buffer, :, keys], dscores[place], ROWS_DOWN)
            query_grad = diagonal(query_grad, heads, dim, per) + edge_ref[unit]
            query_out[at, keys] = query_grad.T
            key_terms = dot(dscores[place], query_masked)
            value_terms = dot(weights[place], grad_masked)
            for slot in range(slots):
                rows = slice(slot * per, (slot + 1) * per)
                terms[entries[slot], :, keys] += key_terms[rows]
                terms[entries[slot], :, values] += value_terms[rows]
        return 0

    lax.fori_loop(0, blocks, block_step, 0)
    copies = [pltpu.make_async_copy(terms.at[pl.ds(0, blocks)], own_terms_ref, out_sems.at[0])]
    copies[0].start()
    count = packed.shape[0]
    chunk = count // 8
    for start in range(0, count, chunk):
        packed[start : start + chunk] = terms[blocks + start : blocks + start + chunk].astype(BF16)
        copy = pltpu.make_async_copy(
            packed.at[pl.ds(start, chunk)],
            returned_ref.at[pl.ds(start, chunk), pl.ds(0, per)],
            out_sems.at[1 + start // chunk],
        )
        copy.start()
        copies.append(copy)
    for copy in copies:
        copy.wait()


def run(kernel, scalars, ins, outs, scratch, estimate, name, mebibytes, elsewhere=()):
    specs = [whole(array.shape) if spec is None else spec for array, spec in ins]
    return pl.pallas_call(
        kernel,
        grid_spec=pltpu.PrefetchScalarGridSpec(
            num_scalar_prefetch=len(scalars),
            grid=(1,),
            in_specs=specs,
            out_specs=[
                ANYWHERE if place in elsewhere else whole(shape) for place, (shape, _) in enumerate(outs)
            ],
            scratch_shapes=scratch,
        ),
        out_shape=[jax.ShapeDtypeStruct(shape, dtype) for shape, dtype in outs],
        compiler_params=params(mebibytes),
        cost_estimate=cost(estimate, 1 << 10),
        name=name,
    )(*scalars, *(array for array, _ in ins))


def forward(scalars, bias, halo, fourth, match_row, far, key_rows, value_rows, query_rows,
            attended_grad, grad_update, out_weight):
    tile_block, tile_count = scalars
    nodes, features = query_rows.shape
    heads = bias.shape[0]
    blocks, slots = tile_count.shape[0], tile_block.shape[0] // tile_count.shape[0]
    per, width = nodes // blocks, features // 2
    columns = heads // 2 * per
    arrays = [match_row, *far, query_rows, attended_grad, grad_update, out_weight]
    return run(
        functools.partial(forward_kernel, heads // 2, features // heads),
        (tile_block, tile_count, bias),
        [(array, ANYWHERE) for array in (halo, key_rows, value_rows, *fourth)] + [(array, None) for array in arrays],
        [
            ((nodes, features), BF16),
            ((8, features // 8, features), BF16),
            ((2 * blocks, 8, columns), F32),
            ((2 * blocks, width, per), F32),
            ((3, 2 * heads, nodes), F32),
        ],
        [
            pltpu.VMEM((blocks + halo.shape[0], per, 2 * features), BF16),
            pltpu.VMEM((1, slots * per, 2 * features), BF16),
            pltpu.VMEM((2, slots * per, columns), F32),
            pltpu.VMEM((2, slots * per, columns), BF16),
            pltpu.VMEM((features, features), F32),
            pltpu.VMEM((nodes, 2 * features), BF16),
            pltpu.VMEM((2 * features, nodes), BF16),
            pltpu.SemaphoreType.DMA((2 * blocks + 1,)),
            pltpu.SemaphoreType.DMA((4,)),
        ],
        FORWARD,
        "forward",
        60,
    )


def fetch_kernel(distance, group_ref, k_below, k_above, v_below, v_above, match_ref, found_ref, rows, sems):
    nodes, both = rows.shape
    features = both // 2
    lanes = (pl.ds(0, features), pl.ds(features, features))
    copies = []
    below_is_partner = lax.rem(group_ref[0] // distance, 2) == 1
    for which, (below, above) in enumerate(((k_below, k_above), (v_below, v_above))):
        target = rows.at[:, lanes[which]]

        @pl.when(below_is_partner)
        def _():
            pltpu.make_async_copy(below, target, sems.at[which]).start()

        @pl.when(jnp.logical_not(below_is_partner))
        def _():
            pltpu.make_async_copy(above, target, sems.at[which]).start()

        copies.append(pltpu.make_async_copy(below, target, sems.at[which]))
    target_node = lax.broadcasted_iota(jnp.int32, (nodes, nodes), 0)
    chosen = (target_node == match_ref[...]).astype(F32).astype(BF16)
    for copy in copies:
        copy.wait()
    found_ref[...] = dot(rows[...], chosen, ROWS_DOWN).astype(BF16)


def fetch(distance, group, arrays, match_row):
    nodes = match_row.shape[1]
    features = arrays[0].shape[1]
    return run(
        functools.partial(fetch_kernel, distance),
        (group,),
        [(array, ANYWHERE) for array in arrays] + [(match_row, None)],
        [((2 * features, nodes), BF16)],
        [pltpu.VMEM((nodes, 2 * features), BF16), pltpu.SemaphoreType.DMA((4,))],
        FETCH,
        "fetch",
        60,
    )[0]


def place_kernel(match_ref, rows_ref, *placed):
    nodes = match_ref.shape[1]
    target_node = lax.broadcasted_iota(jnp.int32, (nodes, nodes), 0)
    for turn, placed_ref in enumerate(placed):
        chosen = (target_node == match_ref[turn : turn + 1, :]).astype(F32).astype(BF16)
        placed_ref[...] = dot(rows_ref[turn].astype(BF16), chosen, ROWS_ACROSS)


def place(matching, rows):
    out = (rows.shape[1:], F32)
    return run(place_kernel, (), [(matching, None), (rows, None)], [out] * 3, [], PLACE, "place", 60)


def backward(scalars, key_rows, value_rows, halo, query_rows, attended_grad, stats, edge_part, spare, heads):
    tile_block, tile_count = scalars
    nodes, features = query_rows.shape
    blocks, slots = tile_count.shape[0], tile_block.shape[0] // tile_count.shape[0]
    per = nodes // blocks
    columns = heads // 2 * per
    count = halo.shape[0]
    return run(
        functools.partial(backward_kernel, heads // 2, features // heads),
        scalars,
        [(key_rows, ANYWHERE), (value_rows, ANYWHERE), (halo, ANYWHERE), (query_rows, None)]
        + [(attended_grad, None), (stats, None), (edge_part, None)],
        [
            ((count, per + spare, 2 * features), BF16),
            ((blocks, per, 2 * features), F32),
            ((nodes, features), F32),
        ],
        [
            pltpu.VMEM((blocks + count, per, 2 * features), BF16),
            pltpu.VMEM((1, slots * per, 2 * features), BF16),
            pltpu.VMEM((BUFFERS, slots * per, columns), BF16),
            pltpu.VMEM((BUFFERS, slots * per, columns), BF16),
            pltpu.VMEM((blocks + count, per, 2 * features), F32),
            pltpu.VMEM((count, per, 2 * features), BF16),
            pltpu.SemaphoreType.DMA((2 * blocks + 1,)),
            pltpu.SemaphoreType.DMA((9,)),
        ],
        BACKWARD,
        "backward",
        60,
        (0, 1),
    )


def collect_kernel(heads, own_ref, *refs):
    placed, edges = refs[:3], refs[3:6]
    key_ref, value_ref = refs[6:]
    blocks, per, both = own_ref.shape
    two = both // 2
    width = two // 2
    dim = width // heads
    for block in range(blocks):
        key_ref[block * per : (block + 1) * per, :] = own_ref[block, :, :two]
        value_ref[block * per : (block + 1) * per, :] = own_ref[block, :, two:]
    row = lax.broadcasted_iota(jnp.int32, (4 * heads, two), 0)
    lane = lax.broadcasted_iota(jnp.int32, (4 * heads, two), 1)
    key_row = (lane // width) * (2 * heads) + lax.rem(lane, width) // dim
    key_spread = (row == key_row).astype(F32).astype(BF16)
    value_spread = (row == key_row + heads).astype(F32).astype(BF16)
    for turn in range(3):
        scalars = edges[turn][...].astype(BF16)
        dscore = dot(scalars, key_spread, ROWS_DOWN)
        weight = dot(scalars, value_spread, ROWS_DOWN)
        key_term = dscore * placed[turn][:, :two].astype(F32)
        value_term = weight * placed[turn][:, two:].astype(F32)
        key_ref[...] += key_term.astype(BF16).astype(F32)
        value_ref[...] += value_term.astype(BF16).astype(F32)


def collect(own, placed, edges, heads):
    blocks, per, both = own.shape
    out = ((blocks * per, both // 2), F32)
    arrays = [own, *placed, *edges]
    return run(
        functools.partial(collect_kernel, heads // 2),
        (),
        [(array, None) for array in arrays],
        [out, out],
        [],
        COLLECT,
        "collect",
        60,
    )


def finish_kernel(send_block, home_ref, key_in, value_in, key_ref, value_ref):
    slots, _, both = home_ref.shape
    two = both // 2
    per = home_ref.shape[1]
    key_ref[...] = key_in[...]
    value_ref[...] = value_in[...]
    for slot in range(slots):
        start = pl.multiple_of(send_block[slot] * per, per)
        key_ref[pl.ds(start, per), :] += home_ref[slot, :, :two].astype(F32)
        value_ref[pl.ds(start, per), :] += home_ref[slot, :, two:].astype(F32)


def finish(send_block, home, key_sum, value_sum, per):
    slots, _, both = home.shape
    out = (key_sum.shape, F32)
    part = pl.BlockSpec((slots, per, both), lambda *_: (0, 0, 0), pipeline_mode=pl.Buffered(1))
    return run(
        finish_kernel,
        (send_block,),
        [(home, part), (key_sum, None), (value_sum, None)],
        [out, out],
        [],
        FINISH,
        "finish",
        60,
    )


def from_partner(array, apart):
    axes = ("group", "dom")
    return lax.ppermute(array, axes, [(i, i ^ 1 << apart) for i in range(lax.axis_size(axes))])


def ahead(array, steps):
    count = lax.axis_size("group")
    return lax.ppermute(array, "group", [(i, (i + steps) % count) for i in range(count)])


def exchange(array, axis):
    return lax.all_to_all(array, axis, split_axis=0, concat_axis=0, tiled=True)


def shards(
    query_rows,
    key_rows,
    value_rows,
    out_weight,
    grad_update,
    expander_bias,
    tile_block,
    tile_count,
    send_block,
    matching,
):
    nodes, features = query_rows.shape
    heads = expander_bias.shape[0]
    tile_block = tile_block[0]
    tile_count = tile_count[0]
    send_block = send_block[0]
    matching = matching[0]
    per = nodes // tile_block.shape[0]
    devices = lax.axis_size(("group", "dom"))
    top_bit = devices.bit_length() - 1
    groups = lax.axis_size("group")

    halo = exchange(outgoing(send_block, key_rows, value_rows, per), "dom")
    attended_grad, *placed = prepare(query_rows, grad_update, out_weight, matching)
    half = nodes // 2
    near = [(ahead(rows, 1), ahead(rows, -1)) for rows in (key_rows, value_rows)]
    near[0], attended_grad = lax.optimization_barrier((near[0], attended_grad))
    group = lax.axis_index("group").astype(jnp.int32).reshape(1)

    def found(turn, distance, ring):
        return fetch(distance, group, [rows for pair in ring for rows in pair], matching[turn : turn + 1])

    next_near = [(ahead(below, 1), ahead(above, -1)) for below, above in near]
    far_2 = found(2, 1, near)
    next_near[1], far_2 = lax.optimization_barrier((next_near[1], far_2))
    third = [(ahead(below[:half], 1), ahead(above[half:], -1)) for below, above in next_near]
    fourth = [(ahead(below, 1), ahead(above, -1)) for below, above in third]
    far_1 = found(1, 2, next_near)
    fourth, far_1, placed[1], placed[2] = lax.optimization_barrier(
        (fourth, far_1, placed[1], placed[2])
    )
    placed = [from_partner(placed[turn], top_bit - 1 - turn) for turn in range(3)]
    fourth = [rows for pair in fourth for rows in pair]

    scalars = (tile_block.reshape(-1), tile_count)
    update, pieces, stats, edge_part, edges = forward(
        scalars, expander_bias, halo, fourth, matching[:1], (far_1, far_2), key_rows, value_rows, query_rows,
        attended_grad, grad_update, out_weight,
    )
    edges = place(matching, edges)
    edges = [from_partner(edges[turn], top_bit - 1 - turn) for turn in range(3)]
    pieces = exchange(pieces, "group")
    spare = features // 8 // 2
    back, own, query_grad = backward(
        scalars, key_rows, value_rows, halo, query_rows, attended_grad, stats, edge_part, spare, heads
    )
    part = pieces.astype(F32).sum(axis=0).astype(BF16)
    part = jnp.concatenate([part[:spare], part[spare:]], axis=1)
    back = back.at[:, per:, :].set(part[None])
    back, placed[1], placed[2] = lax.optimization_barrier((back, placed[1], placed[2]))
    home = exchange(back, "dom")
    key_sum, value_sum = collect(own, placed, edges, heads)
    home, key_sum, value_sum = lax.optimization_barrier((home, key_sum, value_sum))
    key_grad, value_grad = finish(send_block, home, key_sum, value_sum, per)

    summed = home[:, per:, :].astype(F32).sum(axis=0) * (nodes * devices) ** (-0.5)
    summed = jnp.concatenate([summed[:, :features], summed[:, features:]], axis=0)
    copies = jnp.broadcast_to(summed[None], (groups,) + summed.shape)
    weight_grad = exchange(copies, "group").reshape(features, features)
    return (update, query_grad, key_grad, value_grad, weight_grad)


def solution(mesh):
    rows = P(("group", "dom"), None)
    in_specs = (
        rows,
        rows,
        rows,
        P(),
        rows,
        P(),
        P(("group", "dom"), None, None),
        rows,
        rows,
        P(("group", "dom"), None, None),
    )
    out_specs = (rows, rows, rows, rows, P())
    return jax.shard_map(shards, mesh=mesh, in_specs=in_specs, out_specs=out_specs, check_vma=False)
```

```python
import functools

import jax
import jax.numpy as jnp
from jax import lax
from jax.experimental import pallas as pl
from jax.experimental.pallas import tpu as pltpu
from jax.sharding import PartitionSpec as P

F32, BF16 = jnp.float32, jnp.bfloat16
LOG2E = 1.4426950408889634
GATHER, PREPARE, FETCH, FORWARD, BACKWARD, PLACE, COLLECT, FINISH = (
    round(1.15e9 * us) for us in (0.5, 1, 1, 3, 14, 1, 1, 1)
)
BUFFERS = 2
ROWS_ACROSS = (((1,), (1,)), ((), ()))
ROWS_DOWN = (((0,), (0,)), ((), ()))


def whole(shape):
    return pl.BlockSpec(shape, lambda *_: (0,) * len(shape), pipeline_mode=pl.Buffered(1))


ANYWHERE = pl.BlockSpec(memory_space=pl.ANY)


def params(mebibytes=60):
    return pltpu.CompilerParams(vmem_limit_bytes=mebibytes << 20)


def cost(flops, moved):
    return pl.CostEstimate(flops=flops, bytes_accessed=moved, transcendentals=0)


def dot(a, b, dims=(((1,), (0,)), ((), ()))):
    return lax.dot_general(a, b, dims, preferred_element_type=F32)


def gather_kernel(send_block, key_ref, value_ref, sent_ref, rows, sems):
    width = key_ref.shape[1]
    block_rows = sent_ref.shape[1]
    rows[:, :width] = key_ref[...]
    rows[:, width:] = value_ref[...]
    copies = []
    for slot in range(sent_ref.shape[0]):
        start = pl.multiple_of(send_block[slot] * block_rows, block_rows)
        copy = pltpu.make_async_copy(
            rows.at[pl.ds(start, block_rows)], sent_ref.at[slot], sems.at[slot]
        )
        copy.start()
        copies.append(copy)
    for copy in copies:
        copy.wait()


def outgoing(send_block, key_rows, value_rows, block_rows):
    nodes, width = key_rows.shape
    slots = send_block.shape[0]
    return pl.pallas_call(
        gather_kernel,
        grid_spec=pltpu.PrefetchScalarGridSpec(
            num_scalar_prefetch=1,
            grid=(1,),
            in_specs=[whole((nodes, width)), whole((nodes, width))],
            out_specs=pl.BlockSpec(memory_space=pl.ANY),
            scratch_shapes=[
                pltpu.VMEM((nodes, 2 * width), BF16),
                pltpu.SemaphoreType.DMA((slots,)),
            ],
        ),
        out_shape=jax.ShapeDtypeStruct((slots, block_rows, 2 * width), BF16),
        compiler_params=params(),
        cost_estimate=cost(GATHER, 1 << 10),
        name="gather_out",
    )(send_block, key_rows, value_rows)


def prepare_kernel(query_ref, grad_ref, weight_ref, match_ref, attended_ref, *placed):
    nodes, width = query_ref.shape
    grads = dot(grad_ref[...], weight_ref[...], ROWS_ACROSS).astype(BF16)
    attended_ref[...] = grads
    both = jnp.concatenate([query_ref[...], grads], axis=1)
    target = lax.broadcasted_iota(jnp.int32, (nodes, nodes), 0)
    for turn, placed_ref in enumerate(placed):
        chosen = (target == match_ref[turn : turn + 1, :]).astype(F32).astype(BF16)
        placed_ref[...] = dot(chosen, both).astype(BF16)


def prepare(query_rows, grad_update, out_weight, matching):
    nodes, width = query_rows.shape
    turns = matching.shape[0]
    return pl.pallas_call(
        prepare_kernel,
        grid=(1,),
        in_specs=[
            whole((nodes, width)),
            whole((nodes, width)),
            whole((width, width)),
            whole((turns, nodes)),
        ],
        out_specs=[whole((nodes, width))] + [whole((nodes, 2 * width))] * turns,
        out_shape=[jax.ShapeDtypeStruct((nodes, width), BF16)]
        + [jax.ShapeDtypeStruct((nodes, 2 * width), BF16)] * turns,
        compiler_params=params(),
        cost_estimate=cost(1150 * 10**6, 1 << 10),
        name="prepare",
    )(query_rows, grad_update, out_weight, matching)


def head_rows(lanes, heads, per):
    return jnp.concatenate([lanes[:, h * per : (h + 1) * per] for h in range(heads)], axis=0)


def head_lanes(stacked, heads, dim):
    return jnp.concatenate(
        [
            jnp.sum(stacked[h * dim : (h + 1) * dim], axis=0, keepdims=True)
            for h in range(heads)
        ],
        axis=1,
    )


def spread(lanes, heads, dim, per):
    return jnp.concatenate(
        [
            jnp.broadcast_to(lanes[:, h * per : (h + 1) * per], (dim, per))
            for h in range(heads)
        ],
        axis=0,
    )


def diagonal(product, heads, dim, per):
    return jnp.concatenate(
        [
            product[h * dim : (h + 1) * dim, h * per : (h + 1) * per]
            for h in range(heads)
        ],
        axis=0,
    )


def masked_heads(rows, heads, dim):
    lane = lax.broadcasted_iota(jnp.int32, rows.shape, 1) // dim
    wide = rows.astype(F32)
    return jnp.concatenate(
        [jnp.where(lane == h, wide, 0.0) for h in range(heads)], axis=0
    ).astype(BF16)


def fill_table(table, key_ref, value_ref, halo_ref, sems, half=None):
    count = halo_ref.shape[0]
    blocks = table.shape[0] - count
    per, features = table.shape[1], key_ref.shape[1]
    width = features if half is None else features // 2
    first = 0 if half is None else half * width
    copies = []
    for which, ref in enumerate((key_ref, value_ref)):
        target = pl.ds(which * width, width)
        copies.append(
            pltpu.make_async_copy(
                halo_ref.at[:, :, pl.ds(which * features + first, width)],
                table.at[pl.ds(blocks, count), :, target],
                sems.at[2 * blocks + which],
            )
        )
        for block in range(blocks):
            copies.append(
                pltpu.make_async_copy(
                    ref.at[pl.ds(block * per, per), pl.ds(first, width)],
                    table.at[block, :, target],
                    sems.at[2 * block + which],
                )
            )
    for copy in copies:
        copy.start()
    return copies


def live(values, start, rows):
    if start + values.shape[0] <= 5 * values.shape[1] // 4:
        return values
    row = lax.broadcasted_iota(jnp.int32, values.shape, 0) + start
    return jnp.where(row < rows, values, -jnp.inf)


def bring_halves(k_below, k_above, v_below, v_above, rows, sems):
    half, features = k_below.shape
    copies = []
    for which, pair in enumerate(((k_below, k_above), (v_below, v_above))):
        for end, ref in enumerate(pair):
            target = rows.at[pl.ds(end * half, half), pl.ds(which * features, features)]
            copies.append(pltpu.make_async_copy(ref, target, sems.at[2 * end + which]))
    for copy in copies:
        copy.start()
    return copies


def forward_kernel(
    heads, dim, tile_block, tile_count, bias_ref, halo_ref, key_ref, value_ref,
    k_below, k_above, v_below, v_above, match_ref, far_1, far_2, query_ref, grad_ref, update_grad_ref,
    out_weight, update_out, weight_out, stats_out, query_grad_out, edge_out,
    table, picked, scores, raised, weight_sum, rows_4, far_0, sem, sems,
):
    blocks, slots = tile_count.shape[0], tile_block.shape[0] // tile_count.shape[0]
    nodes, features = query_ref.shape
    per = nodes // blocks
    width = heads * dim
    scale = dim**-0.5
    scale2 = scale * LOG2E
    span = slots // 2 * per
    parts = [slice(0, span), slice(span, 2 * span)]
    far = (far_0, far_1, far_2)
    first = bring_halves(k_below, k_above, v_below, v_above, rows_4, sems)
    copies = fill_table(table, key_ref, value_ref, halo_ref, sem)
    target_node = lax.broadcasted_iota(jnp.int32, (nodes, nodes), 0)
    chosen = (target_node == match_ref[...]).astype(F32).astype(BF16)
    for copy in first:
        copy.wait()
    far_0[...] = dot(rows_4[...], chosen, ROWS_DOWN).astype(BF16)
    weight_sum[...] = jnp.zeros_like(weight_sum)
    for copy in copies:
        copy.wait()

    def block_step(step, _):
        buffer = 0
        at = pl.ds(pl.multiple_of(step * per, per), per)
        for slot in range(slots):
            picked[buffer, slot * per : (slot + 1) * per, :] = table[tile_block[step * slots + slot]]
        live_rows = tile_count[step] * per
        query_t = query_ref[at, :].astype(F32).T
        grad_t = grad_ref[at, :].astype(F32).T
        far_keys = [far[turn][:features, at].astype(F32) for turn in range(3)]
        far_values = [far[turn][features:, at].astype(F32) for turn in range(3)]
        attended_t = []
        rows = [[], [], []]
        for half in range(2):
            unit = step * 2 + half
            of = slice(half * width, (half + 1) * width)
            values = slice(features + half * width, features + (half + 1) * width)
            bias = jnp.concatenate(
                [jnp.full((1, per), bias_ref[half * heads + h] * LOG2E, F32) for h in range(heads)],
                axis=1,
            )
            edge_scores = [
                head_lanes(query_t[of] * far_keys[turn][of], heads, dim) * scale2 + bias
                for turn in range(3)
            ]
            query_masked = masked_heads(query_ref[at, of], heads, dim)
            top = None
            for part in parts:
                block = dot(picked[buffer, part, of], query_masked, ROWS_ACROSS)
                block = live(block, part.start, live_rows)
                scores[half, part, :] = block
                part_top = jnp.max(block.reshape(span // 8, 8, heads * per), axis=0)
                top = part_top if top is None else jnp.maximum(top, part_top)
            top = jnp.max(top, axis=0, keepdims=True) * scale2
            for turn in range(3):
                top = jnp.maximum(top, edge_scores[turn])
            total = jnp.zeros((8, heads * per), F32)
            for part in parts:
                block = jnp.exp2(scores[half, part, :] * scale2 - top)
                raised[half, part, :] = block.astype(BF16)
                total = total + jnp.sum(block.reshape(span // 8, 8, heads * per), axis=0)
            total = jnp.sum(total, axis=0, keepdims=True)
            edge_raised = [jnp.exp2(edge_scores[turn] - top) for turn in range(3)]
            total = total + (edge_raised[0] + edge_raised[1] + edge_raised[2])
            inverse = 1.0 / total
            probs = [edge_raised[turn] * inverse for turn in range(3)]
            weights = [probs[turn].astype(BF16).astype(F32) for turn in range(3)]
            mixed = dot(picked[buffer, :, values], raised[half], ROWS_DOWN)
            mixed = diagonal(mixed, heads, dim, per) * spread(inverse, heads, dim, per)
            for turn in range(3):
                mixed = mixed + spread(weights[turn], heads, dim, per) * far_values[turn][of]
            attended = mixed.astype(BF16)
            attended_t.append(attended)
            delta = head_lanes(grad_t[of] * attended.astype(F32), heads, dim)
            stats_out[unit] = jnp.concatenate(
                [top + jnp.log2(total), delta, jnp.zeros((6, heads * per), F32)], axis=0
            )
            query_grad = jnp.zeros((width, per), F32)
            for turn in range(3):
                grad_prob = head_lanes(grad_t[of] * far_values[turn][of], heads, dim)
                dscore = (probs[turn] * (grad_prob - delta) * scale).astype(BF16).astype(F32)
                query_grad = query_grad + spread(dscore, heads, dim, per) * far_keys[turn][of]
                rows[turn] += [head_rows(dscore, heads, per), head_rows(weights[turn], heads, per)]
            query_grad_out[unit] = query_grad
        both = jnp.concatenate(attended_t, axis=0)
        update_out[at, :] = dot(both, out_weight[...], ROWS_DOWN).astype(BF16)
        weight_sum[...] += dot(both, update_grad_ref[at, :])
        for turn in range(3):
            edge_out[turn, :, at] = jnp.concatenate(rows[turn], axis=0)
        return 0

    lax.fori_loop(0, blocks, block_step, 0)
    for piece in range(weight_out.shape[0]):
        rows_each = weight_out.shape[1]
        weight_out[piece] = weight_sum[piece * rows_each : (piece + 1) * rows_each, :].astype(BF16)


def backward_kernel(
    half, heads, dim, tile_block, tile_count, key_ref, value_ref, halo_ref, query_ref, grad_ref,
    stats_ref, edge_ref, returned_ref, own_terms_ref, query_out,
    table, picked, weights, dscores, terms, packed, sem, out_sems,
):
    blocks, slots = tile_count.shape[0], tile_block.shape[0] // tile_count.shape[0]
    nodes = query_ref.shape[0]
    per = nodes // blocks
    width = heads * dim
    scale = dim**-0.5
    scale2 = scale * LOG2E
    span = slots // 2 * per
    parts = [slice(0, span), slice(span, 2 * span)]
    copies = fill_table(table, key_ref, value_ref, halo_ref, sem, half)
    terms[...] = jnp.zeros_like(terms)
    for copy in copies:
        copy.wait()

    def block_step(step, _):
        buffer = 0
        at = pl.ds(pl.multiple_of(step * per, per), per)
        entries = [tile_block[step * slots + slot] for slot in range(slots)]
        for slot in range(slots):
            picked[buffer, slot * per : (slot + 1) * per, :] = table[entries[slot]]
        live_rows = tile_count[step] * per
        unit = step * 2 + half
        place = 0
        keys = slice(0, width)
        values = slice(width, 2 * width)
        query_masked = masked_heads(query_ref[at, :], heads, dim)
        grad_masked = masked_heads(grad_ref[at, :], heads, dim)
        log_total, delta = stats_ref[unit, 0:1, :], stats_ref[unit, 1:2, :]
        for part in parts:
            block = dot(picked[buffer, part, keys], query_masked, ROWS_ACROSS)
            block = live(block, part.start, live_rows)
            prob = jnp.exp2(block * scale2 - log_total)
            weights[place, part, :] = prob.astype(BF16)
            grad_prob = dot(picked[buffer, part, values], grad_masked, ROWS_ACROSS)
            dscores[place, part, :] = (prob * scale * (grad_prob - delta)).astype(BF16)
        query_grad = dot(picked[buffer, :, keys], dscores[place], ROWS_DOWN)
        query_grad = diagonal(query_grad, heads, dim, per) + edge_ref[unit]
        query_out[at, :] = query_grad.T
        key_terms = dot(dscores[place], query_masked)
        value_terms = dot(weights[place], grad_masked)
        for slot in range(slots):
            rows = slice(slot * per, (slot + 1) * per)
            terms[entries[slot], :, keys] += key_terms[rows]
            terms[entries[slot], :, values] += value_terms[rows]
        return 0

    lax.fori_loop(0, blocks, block_step, 0)
    copies = [pltpu.make_async_copy(terms.at[pl.ds(0, blocks)], own_terms_ref, out_sems.at[0])]
    copies[0].start()
    count = packed.shape[0]
    chunk = count // 8
    for start in range(0, count, chunk):
        packed[start : start + chunk] = terms[blocks + start : blocks + start + chunk].astype(BF16)
        copy = pltpu.make_async_copy(
            packed.at[pl.ds(start, chunk)],
            returned_ref.at[pl.ds(start, chunk), pl.ds(0, per)],
            out_sems.at[1 + start // chunk],
        )
        copy.start()
        copies.append(copy)
    for copy in copies:
        copy.wait()


def run(kernel, scalars, ins, outs, scratch, estimate, name, mebibytes, elsewhere=()):
    specs = [whole(array.shape) if spec is None else spec for array, spec in ins]
    return pl.pallas_call(
        kernel,
        grid_spec=pltpu.PrefetchScalarGridSpec(
            num_scalar_prefetch=len(scalars),
            grid=(1,),
            in_specs=specs,
            out_specs=[
                ANYWHERE if place in elsewhere else whole(shape) for place, (shape, _) in enumerate(outs)
            ],
            scratch_shapes=scratch,
        ),
        out_shape=[jax.ShapeDtypeStruct(shape, dtype) for shape, dtype in outs],
        compiler_params=params(mebibytes),
        cost_estimate=cost(estimate, 1 << 10),
        name=name,
    )(*scalars, *(array for array, _ in ins))


def forward(scalars, bias, halo, fourth, match_row, far, key_rows, value_rows, query_rows,
            attended_grad, grad_update, out_weight):
    tile_block, tile_count = scalars
    nodes, features = query_rows.shape
    heads = bias.shape[0]
    blocks, slots = tile_count.shape[0], tile_block.shape[0] // tile_count.shape[0]
    per, width = nodes // blocks, features // 2
    columns = heads // 2 * per
    arrays = [match_row, *far, query_rows, attended_grad, grad_update, out_weight]
    return run(
        functools.partial(forward_kernel, heads // 2, features // heads),
        (tile_block, tile_count, bias),
        [(array, ANYWHERE) for array in (halo, key_rows, value_rows, *fourth)] + [(array, None) for array in arrays],
        [
            ((nodes, features), BF16),
            ((8, features // 8, features), BF16),
            ((2 * blocks, 8, columns), F32),
            ((2 * blocks, width, per), F32),
            ((3, 2 * heads, nodes), F32),
        ],
        [
            pltpu.VMEM((blocks + halo.shape[0], per, 2 * features), BF16),
            pltpu.VMEM((1, slots * per, 2 * features), BF16),
            pltpu.VMEM((2, slots * per, columns), F32),
            pltpu.VMEM((2, slots * per, columns), BF16),
            pltpu.VMEM((features, features), F32),
            pltpu.VMEM((nodes, 2 * features), BF16),
            pltpu.VMEM((2 * features, nodes), BF16),
            pltpu.SemaphoreType.DMA((2 * blocks + 2,)),
            pltpu.SemaphoreType.DMA((4,)),
        ],
        FORWARD,
        "forward",
        60,
    )


def fetch_kernel(distance, group_ref, k_below, k_above, v_below, v_above, match_ref, found_ref, rows, sems):
    nodes, both = rows.shape
    features = both // 2
    lanes = (pl.ds(0, features), pl.ds(features, features))
    copies = []
    below_is_partner = lax.rem(group_ref[0] // distance, 2) == 1
    for which, (below, above) in enumerate(((k_below, k_above), (v_below, v_above))):
        target = rows.at[:, lanes[which]]

        @pl.when(below_is_partner)
        def _():
            pltpu.make_async_copy(below, target, sems.at[which]).start()

        @pl.when(jnp.logical_not(below_is_partner))
        def _():
            pltpu.make_async_copy(above, target, sems.at[which]).start()

        copies.append(pltpu.make_async_copy(below, target, sems.at[which]))
    target_node = lax.broadcasted_iota(jnp.int32, (nodes, nodes), 0)
    chosen = (target_node == match_ref[...]).astype(F32).astype(BF16)
    for copy in copies:
        copy.wait()
    found_ref[...] = dot(rows[...], chosen, ROWS_DOWN).astype(BF16)


def fetch(distance, group, arrays, match_row):
    nodes = match_row.shape[1]
    features = arrays[0].shape[1]
    return run(
        functools.partial(fetch_kernel, distance),
        (group,),
        [(array, ANYWHERE) for array in arrays] + [(match_row, None)],
        [((2 * features, nodes), BF16)],
        [pltpu.VMEM((nodes, 2 * features), BF16), pltpu.SemaphoreType.DMA((4,))],
        FETCH,
        "fetch",
        60,
    )[0]


def place_kernel(match_ref, rows_ref, *placed):
    nodes = match_ref.shape[1]
    target_node = lax.broadcasted_iota(jnp.int32, (nodes, nodes), 0)
    for turn, placed_ref in enumerate(placed):
        chosen = (target_node == match_ref[turn : turn + 1, :]).astype(F32).astype(BF16)
        placed_ref[...] = dot(rows_ref[turn].astype(BF16), chosen, ROWS_ACROSS)


def place(matching, rows):
    out = (rows.shape[1:], F32)
    return run(place_kernel, (), [(matching, None), (rows, None)], [out] * 3, [], PLACE, "place", 60)


def backward(half, scalars, key_rows, value_rows, halo, query_rows, attended_grad, stats, edge_part, spare, heads):
    tile_block, tile_count = scalars
    nodes, features = query_rows.shape
    blocks, slots = tile_count.shape[0], tile_block.shape[0] // tile_count.shape[0]
    per, width = nodes // blocks, features // 2
    columns = heads // 2 * per
    count = halo.shape[0]
    part = pl.BlockSpec((nodes, width), lambda *_: (0, half), pipeline_mode=pl.Buffered(1))
    return run(
        functools.partial(backward_kernel, half, heads // 2, features // heads),
        scalars,
        [(key_rows, ANYWHERE), (value_rows, ANYWHERE), (halo, ANYWHERE), (query_rows, part)]
        + [(attended_grad, part), (stats, None), (edge_part, None)],
        [
            ((count, per + spare, features), BF16),
            ((blocks, per, features), F32),
            ((nodes, width), F32),
        ],
        [
            pltpu.VMEM((blocks + count, per, features), BF16),
            pltpu.VMEM((1, slots * per, features), BF16),
            pltpu.VMEM((1, slots * per, columns), BF16),
            pltpu.VMEM((1, slots * per, columns), BF16),
            pltpu.VMEM((blocks + count, per, features), F32),
            pltpu.VMEM((count, per, features), BF16),
            pltpu.SemaphoreType.DMA((2 * blocks + 2,)),
            pltpu.SemaphoreType.DMA((9,)),
        ],
        BACKWARD,
        "backward",
        60,
        (0, 1),
    )


def add_home(send_block, home_ref, key_ref, value_ref, width):
    per = home_ref.shape[1]
    for slot in range(home_ref.shape[0]):
        rows = pl.ds(pl.multiple_of(send_block[slot] * per, per), per)
        key_ref[rows, :width] += home_ref[slot, :, :width].astype(F32)
        value_ref[rows, :width] += home_ref[slot, :, width:].astype(F32)


def collect_kernel(heads, send_block, own_a, own_b, home_ref, *refs):
    placed, edges = refs[:3], refs[3:6]
    key_ref, value_ref = refs[6:]
    blocks, per, two = own_a.shape
    width = two // 2
    dim = width // heads
    for block in range(blocks):
        at = slice(block * per, (block + 1) * per)
        key_ref[at, :width] = own_a[block, :, :width]
        key_ref[at, width:] = own_b[block, :, :width]
        value_ref[at, :width] = own_a[block, :, width:]
        value_ref[at, width:] = own_b[block, :, width:]
    row = lax.broadcasted_iota(jnp.int32, (4 * heads, two), 0)
    lane = lax.broadcasted_iota(jnp.int32, (4 * heads, two), 1)
    key_row = (lane // width) * (2 * heads) + lax.rem(lane, width) // dim
    key_spread = (row == key_row).astype(F32).astype(BF16)
    value_spread = (row == key_row + heads).astype(F32).astype(BF16)
    for turn in range(3):
        scalars = edges[turn][...].astype(BF16)
        dscore = dot(scalars, key_spread, ROWS_DOWN)
        weight = dot(scalars, value_spread, ROWS_DOWN)
        key_term = dscore * placed[turn][:, :two].astype(F32)
        value_term = weight * placed[turn][:, two:].astype(F32)
        key_ref[...] += key_term.astype(BF16).astype(F32)
        value_ref[...] += value_term.astype(BF16).astype(F32)
    add_home(send_block, home_ref, key_ref, value_ref, width)


def collect(send_block, own_a, own_b, home, placed, edges, heads):
    blocks, per, two = own_a.shape
    slots = home.shape[0]
    out = ((blocks * per, two), F32)
    part = pl.BlockSpec((slots, per, two), lambda *_: (0, 0, 0), pipeline_mode=pl.Buffered(1))
    return run(
        functools.partial(collect_kernel, heads // 2),
        (send_block,),
        [(own_a, None), (own_b, None), (home, part)] + [(array, None) for array in (*placed, *edges)],
        [out, out],
        [],
        COLLECT,
        "collect",
        60,
    )


def finish_kernel(send_block, home_ref, key_in, value_in, key_ref, value_ref):
    key_ref[...] = key_in[...]
    value_ref[...] = value_in[...]
    add_home(send_block, home_ref, key_ref, value_ref, key_ref.shape[1])


def finish(send_block, home, key_sum, value_sum):
    nodes, two = key_sum.shape
    half = pl.BlockSpec((nodes, two // 2), lambda *_: (0, 1), pipeline_mode=pl.Buffered(1))
    return pl.pallas_call(
        finish_kernel,
        grid_spec=pltpu.PrefetchScalarGridSpec(
            num_scalar_prefetch=1,
            grid=(1,),
            in_specs=[whole(home.shape), half, half],
            out_specs=[half, half],
        ),
        out_shape=[jax.ShapeDtypeStruct((nodes, two), F32)] * 2,
        input_output_aliases={2: 0, 3: 1},
        compiler_params=params(),
        cost_estimate=cost(FINISH, 1 << 10),
        name="finish",
    )(send_block, home, key_sum, value_sum)


def from_partner(array, apart):
    axes = ("group", "dom")
    return lax.ppermute(array, axes, [(i, i ^ 1 << apart) for i in range(lax.axis_size(axes))])


def ahead(array, steps):
    count = lax.axis_size("group")
    return lax.ppermute(array, "group", [(i, (i + steps) % count) for i in range(count)])


def across(array, axis, apart):
    return lax.ppermute(array, axis, [(i, i ^ apart) for i in range(lax.axis_size(axis))])


def exchange(array, axis):
    return lax.all_to_all(array, axis, split_axis=0, concat_axis=0, tiled=True)


def shards(
    query_rows,
    key_rows,
    value_rows,
    out_weight,
    grad_update,
    expander_bias,
    tile_block,
    tile_count,
    send_block,
    matching,
):
    nodes, features = query_rows.shape
    heads = expander_bias.shape[0]
    tile_block = tile_block[0]
    tile_count = tile_count[0]
    send_block = send_block[0]
    matching = matching[0]
    per = nodes // tile_block.shape[0]
    devices = lax.axis_size(("group", "dom"))
    top_bit = devices.bit_length() - 1
    groups = lax.axis_size("group")

    halo = exchange(outgoing(send_block, key_rows, value_rows, per), "dom")
    attended_grad, *placed = prepare(query_rows, grad_update, out_weight, matching)
    half = nodes // 2
    near = [(ahead(rows, 1), ahead(rows, -1)) for rows in (key_rows, value_rows)]
    near[0], attended_grad = lax.optimization_barrier((near[0], attended_grad))
    group = lax.axis_index("group").astype(jnp.int32).reshape(1)

    def found(turn, distance, ring):
        return fetch(distance, group, [rows for pair in ring for rows in pair], matching[turn : turn + 1])

    next_near = [(ahead(below, 1), ahead(above, -1)) for below, above in near]
    far_2 = found(2, 1, near)
    next_near[1], far_2 = lax.optimization_barrier((next_near[1], far_2))
    third = [(ahead(below[:half], 1), ahead(above[half:], -1)) for below, above in next_near]
    fourth = [(ahead(below, 1), ahead(above, -1)) for below, above in third]
    far_1 = found(1, 2, next_near)
    fourth, far_1, placed[1], placed[2] = lax.optimization_barrier(
        (fourth, far_1, placed[1], placed[2])
    )
    placed = [from_partner(placed[turn], top_bit - 1 - turn) for turn in range(3)]
    fourth = [rows for pair in fourth for rows in pair]

    scalars = (tile_block.reshape(-1), tile_count)
    update, pieces, stats, edge_part, edges = forward(
        scalars, expander_bias, halo, fourth, matching[:1], (far_1, far_2), key_rows, value_rows, query_rows,
        attended_grad, grad_update, out_weight,
    )
    pieces = exchange(pieces, "group")
    spare = features // groups
    common = (scalars, key_rows, value_rows, halo, query_rows, attended_grad)
    back_a, own_a, query_a = backward(0, *common, stats, edge_part, spare, heads)
    part = pieces.astype(F32).sum(axis=0).astype(BF16)
    back_a = back_a.at[:, per:, :].set(part[None])
    back_a, placed[1], placed[2] = lax.optimization_barrier((back_a, placed[1], placed[2]))
    home_a = exchange(back_a, "dom")
    back_b, own_b, query_b = backward(1, *common, stats, edge_part, 0, heads)
    back_b, home_a, edges, placed[0] = lax.optimization_barrier((back_b, home_a, edges, placed[0]))
    edges = place(matching, edges)
    edges = [from_partner(edges[turn], top_bit - 1 - turn) for turn in range(3)]
    home_b = exchange(back_b, "dom")
    query_grad = jnp.concatenate([query_a, query_b], axis=1)

    weight_grad = home_a[:, per:, :].astype(F32).sum(axis=0) * (nodes * devices) ** (-0.5)
    apart = 1
    while apart < groups:
        other = across(weight_grad, "group", apart)
        upper = lax.rem(group[0] // apart, 2) == 1
        weight_grad = jnp.where(
            upper, jnp.concatenate([other, weight_grad]), jnp.concatenate([weight_grad, other])
        )
        apart *= 2
    key_sum, value_sum = collect(send_block, own_a, own_b, home_a, placed, edges, heads)
    home_b, key_sum, value_sum, weight_grad, query_grad = lax.optimization_barrier(
        (home_b, key_sum, value_sum, weight_grad, query_grad)
    )
    key_grad, value_grad = finish(send_block, home_b, key_sum, value_sum)
    return (update, query_grad, key_grad, value_grad, weight_grad)


def solution(mesh):
    rows = P(("group", "dom"), None)
    in_specs = (
        rows,
        rows,
        rows,
        P(),
        rows,
        P(),
        P(("group", "dom"), None, None),
        rows,
        rows,
        P(("group", "dom"), None, None),
    )
    out_specs = (rows, rows, rows, rows, P())
    return jax.shard_map(shards, mesh=mesh, in_specs=in_specs, out_specs=out_specs, check_vma=False)
```

```python
import functools

import jax
import jax.numpy as jnp
from jax import lax
from jax.experimental import pallas as pl
from jax.experimental.pallas import tpu as pltpu
from jax.sharding import PartitionSpec as P

F32, BF16 = jnp.float32, jnp.bfloat16
LOG2E = 1.4426950408889634
GATHER, PREPARE, FETCH, FORWARD, BACKWARD, PLACE, COLLECT, FINISH = (
    round(1.15e9 * us) for us in (0.5, 1, 1, 3, 14, 1, 1, 1)
)
BUFFERS = 2
ROWS_ACROSS = (((1,), (1,)), ((), ()))
ROWS_DOWN = (((0,), (0,)), ((), ()))


def whole(shape):
    return pl.BlockSpec(shape, lambda *_: (0,) * len(shape), pipeline_mode=pl.Buffered(1))


ANYWHERE = pl.BlockSpec(memory_space=pl.ANY)


def params(mebibytes=60):
    return pltpu.CompilerParams(vmem_limit_bytes=mebibytes << 20)


def cost(flops, moved):
    return pl.CostEstimate(flops=flops, bytes_accessed=moved, transcendentals=0)


def dot(a, b, dims=(((1,), (0,)), ((), ()))):
    return lax.dot_general(a, b, dims, preferred_element_type=F32)


def gather_kernel(send_block, key_ref, value_ref, sent_ref, rows, sems):
    width = key_ref.shape[1]
    block_rows = sent_ref.shape[1]
    rows[:, :width] = key_ref[...]
    rows[:, width:] = value_ref[...]
    copies = []
    for slot in range(sent_ref.shape[0]):
        start = pl.multiple_of(send_block[slot] * block_rows, block_rows)
        copy = pltpu.make_async_copy(
            rows.at[pl.ds(start, block_rows)], sent_ref.at[slot], sems.at[slot]
        )
        copy.start()
        copies.append(copy)
    for copy in copies:
        copy.wait()


def outgoing(send_block, key_rows, value_rows, block_rows):
    nodes, width = key_rows.shape
    slots = send_block.shape[0]
    return pl.pallas_call(
        gather_kernel,
        grid_spec=pltpu.PrefetchScalarGridSpec(
            num_scalar_prefetch=1,
            grid=(1,),
            in_specs=[whole((nodes, width)), whole((nodes, width))],
            out_specs=pl.BlockSpec(memory_space=pl.ANY),
            scratch_shapes=[
                pltpu.VMEM((nodes, 2 * width), BF16),
                pltpu.SemaphoreType.DMA((slots,)),
            ],
        ),
        out_shape=jax.ShapeDtypeStruct((slots, block_rows, 2 * width), BF16),
        compiler_params=params(),
        cost_estimate=cost(GATHER, 1 << 10),
        name="gather_out",
    )(send_block, key_rows, value_rows)


def prepare_kernel(query_ref, grad_ref, weight_ref, match_ref, attended_ref, *placed):
    nodes, width = query_ref.shape
    grads = dot(grad_ref[...], weight_ref[...], ROWS_ACROSS).astype(BF16)
    attended_ref[...] = grads
    both = jnp.concatenate([query_ref[...], grads], axis=1)
    target = lax.broadcasted_iota(jnp.int32, (nodes, nodes), 0)
    for turn, placed_ref in enumerate(placed):
        chosen = (target == match_ref[turn : turn + 1, :]).astype(F32).astype(BF16)
        placed_ref[...] = dot(chosen, both).astype(BF16)


def prepare(query_rows, grad_update, out_weight, matching):
    nodes, width = query_rows.shape
    turns = matching.shape[0]
    return pl.pallas_call(
        prepare_kernel,
        grid=(1,),
        in_specs=[
            whole((nodes, width)),
            whole((nodes, width)),
            whole((width, width)),
            whole((turns, nodes)),
        ],
        out_specs=[whole((nodes, width))] + [whole((nodes, 2 * width))] * turns,
        out_shape=[jax.ShapeDtypeStruct((nodes, width), BF16)]
        + [jax.ShapeDtypeStruct((nodes, 2 * width), BF16)] * turns,
        compiler_params=params(),
        cost_estimate=cost(1150 * 10**6, 1 << 10),
        name="prepare",
    )(query_rows, grad_update, out_weight, matching)


def head_rows(lanes, heads, per):
    return jnp.concatenate([lanes[:, h * per : (h + 1) * per] for h in range(heads)], axis=0)


def head_lanes(stacked, heads, dim):
    return jnp.concatenate(
        [
            jnp.sum(stacked[h * dim : (h + 1) * dim], axis=0, keepdims=True)
            for h in range(heads)
        ],
        axis=1,
    )


def spread(lanes, heads, dim, per):
    return jnp.concatenate(
        [
            jnp.broadcast_to(lanes[:, h * per : (h + 1) * per], (dim, per))
            for h in range(heads)
        ],
        axis=0,
    )


def diagonal(product, heads, dim, per):
    return jnp.concatenate(
        [
            product[h * dim : (h + 1) * dim, h * per : (h + 1) * per]
            for h in range(heads)
        ],
        axis=0,
    )


def masked_heads(rows, heads, dim):
    lane = lax.broadcasted_iota(jnp.int32, rows.shape, 1) // dim
    wide = rows.astype(F32)
    return jnp.concatenate(
        [jnp.where(lane == h, wide, 0.0) for h in range(heads)], axis=0
    ).astype(BF16)


def fill_table(table, key_ref, value_ref, halo_ref, sems, half=None):
    count = halo_ref.shape[0]
    blocks = table.shape[0] - count
    per, features = table.shape[1], key_ref.shape[1]
    width = features if half is None else features // 2
    first = 0 if half is None else half * width
    copies = []
    for which, ref in enumerate((key_ref, value_ref)):
        target = pl.ds(which * width, width)
        copies.append(
            pltpu.make_async_copy(
                halo_ref.at[:, :, pl.ds(which * features + first, width)],
                table.at[pl.ds(blocks, count), :, target],
                sems.at[2 * blocks + which],
            )
        )
        for block in range(blocks):
            copies.append(
                pltpu.make_async_copy(
                    ref.at[pl.ds(block * per, per), pl.ds(first, width)],
                    table.at[block, :, target],
                    sems.at[2 * block + which],
                )
            )
    for copy in copies:
        copy.start()
    return copies


def live(values, start, rows):
    if start + values.shape[0] <= 5 * values.shape[1] // 4:
        return values
    row = lax.broadcasted_iota(jnp.int32, values.shape, 0) + start
    return jnp.where(row < rows, values, -jnp.inf)


def bring_halves(k_below, k_above, v_below, v_above, rows, sems):
    half, features = k_below.shape
    copies = []
    for which, pair in enumerate(((k_below, k_above), (v_below, v_above))):
        for end, ref in enumerate(pair):
            target = rows.at[pl.ds(end * half, half), pl.ds(which * features, features)]
            copies.append(pltpu.make_async_copy(ref, target, sems.at[2 * end + which]))
    for copy in copies:
        copy.start()
    return copies


def forward_kernel(
    heads, dim, tile_block, tile_count, bias_ref, halo_ref, key_ref, value_ref,
    k_below, k_above, v_below, v_above, match_ref, far_1, far_2, query_ref, grad_ref, update_grad_ref,
    out_weight, update_out, weight_out, stats_out, query_grad_out, edge_out,
    table, picked, scores, raised, weight_sum, rows_4, far_0, sem, sems,
):
    blocks, slots = tile_count.shape[0], tile_block.shape[0] // tile_count.shape[0]
    nodes, features = query_ref.shape
    per = nodes // blocks
    width = heads * dim
    scale = dim**-0.5
    scale2 = scale * LOG2E
    span = slots // 2 * per
    parts = [slice(0, span), slice(span, 2 * span)]
    far = (far_0, far_1, far_2)
    first = bring_halves(k_below, k_above, v_below, v_above, rows_4, sems)
    copies = fill_table(table, key_ref, value_ref, halo_ref, sem)
    target_node = lax.broadcasted_iota(jnp.int32, (nodes, nodes), 0)
    chosen = (target_node == match_ref[...]).astype(F32).astype(BF16)
    for copy in first:
        copy.wait()
    far_0[...] = dot(rows_4[...], chosen, ROWS_DOWN).astype(BF16)
    weight_sum[...] = jnp.zeros_like(weight_sum)
    for copy in copies:
        copy.wait()

    def block_step(step, _):
        buffer = 0
        at = pl.ds(pl.multiple_of(step * per, per), per)
        for slot in range(slots):
            picked[buffer, slot * per : (slot + 1) * per, :] = table[tile_block[step * slots + slot]]
        live_rows = tile_count[step] * per
        query_t = query_ref[at, :].astype(F32).T
        grad_t = grad_ref[at, :].astype(F32).T
        far_keys = [far[turn][:features, at].astype(F32) for turn in range(3)]
        far_values = [far[turn][features:, at].astype(F32) for turn in range(3)]
        attended_t = []
        rows = [[], [], []]
        for half in range(2):
            unit = step * 2 + half
            of = slice(half * width, (half + 1) * width)
            values = slice(features + half * width, features + (half + 1) * width)
            bias = jnp.concatenate(
                [jnp.full((1, per), bias_ref[half * heads + h] * LOG2E, F32) for h in range(heads)],
                axis=1,
            )
            edge_scores = [
                head_lanes(query_t[of] * far_keys[turn][of], heads, dim) * scale2 + bias
                for turn in range(3)
            ]
            query_masked = masked_heads(query_ref[at, of], heads, dim)
            top = None
            for part in parts:
                block = dot(picked[buffer, part, of], query_masked, ROWS_ACROSS)
                block = live(block, part.start, live_rows)
                scores[half, part, :] = block
                part_top = jnp.max(block.reshape(span // 8, 8, heads * per), axis=0)
                top = part_top if top is None else jnp.maximum(top, part_top)
            top = jnp.max(top, axis=0, keepdims=True) * scale2
            for turn in range(3):
                top = jnp.maximum(top, edge_scores[turn])
            total = jnp.zeros((8, heads * per), F32)
            for part in parts:
                block = jnp.exp2(scores[half, part, :] * scale2 - top)
                raised[half, part, :] = block.astype(BF16)
                total = total + jnp.sum(block.reshape(span // 8, 8, heads * per), axis=0)
            total = jnp.sum(total, axis=0, keepdims=True)
            edge_raised = [jnp.exp2(edge_scores[turn] - top) for turn in range(3)]
            total = total + (edge_raised[0] + edge_raised[1] + edge_raised[2])
            inverse = 1.0 / total
            probs = [edge_raised[turn] * inverse for turn in range(3)]
            weights = [probs[turn].astype(BF16).astype(F32) for turn in range(3)]
            mixed = dot(picked[buffer, :, values], raised[half], ROWS_DOWN)
            mixed = diagonal(mixed, heads, dim, per) * spread(inverse, heads, dim, per)
            for turn in range(3):
                mixed = mixed + spread(weights[turn], heads, dim, per) * far_values[turn][of]
            attended = mixed.astype(BF16)
            attended_t.append(attended)
            delta = head_lanes(grad_t[of] * attended.astype(F32), heads, dim)
            stats_out[unit] = jnp.concatenate(
                [top + jnp.log2(total), delta, jnp.zeros((6, heads * per), F32)], axis=0
            )
            query_grad = jnp.zeros((width, per), F32)
            for turn in range(3):
                grad_prob = head_lanes(grad_t[of] * far_values[turn][of], heads, dim)
                dscore = (probs[turn] * (grad_prob - delta) * scale).astype(BF16).astype(F32)
                query_grad = query_grad + spread(dscore, heads, dim, per) * far_keys[turn][of]
                rows[turn] += [head_rows(dscore, heads, per), head_rows(weights[turn], heads, per)]
            query_grad_out[unit] = query_grad
        both = jnp.concatenate(attended_t, axis=0)
        update_out[at, :] = dot(both, out_weight[...], ROWS_DOWN).astype(BF16)
        weight_sum[...] += dot(both, update_grad_ref[at, :])
        for turn in range(3):
            edge_out[turn, :, at] = jnp.concatenate(rows[turn], axis=0)
        return 0

    lax.fori_loop(0, blocks, block_step, 0)
    for piece in range(weight_out.shape[0]):
        rows_each = weight_out.shape[1]
        weight_out[piece] = weight_sum[piece * rows_each : (piece + 1) * rows_each, :].astype(BF16)


def backward_kernel(
    half, heads, dim, tile_block, tile_count, key_ref, value_ref, halo_ref, query_ref, grad_ref,
    stats_ref, edge_ref, returned_ref, own_terms_ref, query_out,
    table, picked, weights, dscores, terms, packed, sem, out_sems,
):
    blocks, slots = tile_count.shape[0], tile_block.shape[0] // tile_count.shape[0]
    nodes = query_ref.shape[0]
    per = nodes // blocks
    width = heads * dim
    scale = dim**-0.5
    scale2 = scale * LOG2E
    span = slots // 2 * per
    parts = [slice(0, span), slice(span, 2 * span)]
    copies = fill_table(table, key_ref, value_ref, halo_ref, sem, half)
    terms[...] = jnp.zeros_like(terms)
    for copy in copies:
        copy.wait()

    def block_step(step, _):
        buffer = 0
        at = pl.ds(pl.multiple_of(step * per, per), per)
        entries = [tile_block[step * slots + slot] for slot in range(slots)]
        for slot in range(slots):
            picked[buffer, slot * per : (slot + 1) * per, :] = table[entries[slot]]
        live_rows = tile_count[step] * per
        unit = step * 2 + half
        place = 0
        keys = slice(0, width)
        values = slice(width, 2 * width)
        query_masked = masked_heads(query_ref[at, :], heads, dim)
        grad_masked = masked_heads(grad_ref[at, :], heads, dim)
        log_total, delta = stats_ref[unit, 0:1, :], stats_ref[unit, 1:2, :]
        for part in parts:
            block = dot(picked[buffer, part, keys], query_masked, ROWS_ACROSS)
            block = live(block, part.start, live_rows)
            prob = jnp.exp2(block * scale2 - log_total)
            weights[place, part, :] = prob.astype(BF16)
            grad_prob = dot(picked[buffer, part, values], grad_masked, ROWS_ACROSS)
            dscores[place, part, :] = (prob * scale * (grad_prob - delta)).astype(BF16)
        query_grad = dot(picked[buffer, :, keys], dscores[place], ROWS_DOWN)
        query_grad = diagonal(query_grad, heads, dim, per) + edge_ref[unit]
        query_out[at, :] = query_grad.T
        key_terms = dot(dscores[place], query_masked)
        value_terms = dot(weights[place], grad_masked)
        for slot in range(slots):
            rows = slice(slot * per, (slot + 1) * per)
            terms[entries[slot], :, keys] += key_terms[rows]
            terms[entries[slot], :, values] += value_terms[rows]
        return 0

    lax.fori_loop(0, blocks, block_step, 0)
    copies = [pltpu.make_async_copy(terms.at[pl.ds(0, blocks)], own_terms_ref, out_sems.at[0])]
    copies[0].start()
    count = packed.shape[0]
    chunk = count // 8
    for start in range(0, count, chunk):
        packed[start : start + chunk] = terms[blocks + start : blocks + start + chunk].astype(BF16)
        copy = pltpu.make_async_copy(
            packed.at[pl.ds(start, chunk)],
            returned_ref.at[pl.ds(start, chunk), pl.ds(0, per)],
            out_sems.at[1 + start // chunk],
        )
        copy.start()
        copies.append(copy)
    for copy in copies:
        copy.wait()


def run(kernel, scalars, ins, outs, scratch, estimate, name, mebibytes, elsewhere=()):
    specs = [whole(array.shape) if spec is None else spec for array, spec in ins]
    return pl.pallas_call(
        kernel,
        grid_spec=pltpu.PrefetchScalarGridSpec(
            num_scalar_prefetch=len(scalars),
            grid=(1,),
            in_specs=specs,
            out_specs=[
                ANYWHERE if place in elsewhere else whole(shape) for place, (shape, _) in enumerate(outs)
            ],
            scratch_shapes=scratch,
        ),
        out_shape=[jax.ShapeDtypeStruct(shape, dtype) for shape, dtype in outs],
        compiler_params=params(mebibytes),
        cost_estimate=cost(estimate, 1 << 10),
        name=name,
    )(*scalars, *(array for array, _ in ins))


def forward(scalars, bias, halo, fourth, match_row, far, key_rows, value_rows, query_rows,
            attended_grad, grad_update, out_weight):
    tile_block, tile_count = scalars
    nodes, features = query_rows.shape
    heads = bias.shape[0]
    blocks, slots = tile_count.shape[0], tile_block.shape[0] // tile_count.shape[0]
    per, width = nodes // blocks, features // 2
    columns = heads // 2 * per
    arrays = [match_row, *far, query_rows, attended_grad, grad_update, out_weight]
    return run(
        functools.partial(forward_kernel, heads // 2, features // heads),
        (tile_block, tile_count, bias),
        [(array, ANYWHERE) for array in (halo, key_rows, value_rows, *fourth)] + [(array, None) for array in arrays],
        [
            ((nodes, features), BF16),
            ((8, features // 8, features), BF16),
            ((2 * blocks, 8, columns), F32),
            ((2 * blocks, width, per), F32),
            ((3, 2 * heads, nodes), F32),
        ],
        [
            pltpu.VMEM((blocks + halo.shape[0], per, 2 * features), BF16),
            pltpu.VMEM((1, slots * per, 2 * features), BF16),
            pltpu.VMEM((2, slots * per, columns), F32),
            pltpu.VMEM((2, slots * per, columns), BF16),
            pltpu.VMEM((features, features), F32),
            pltpu.VMEM((nodes, 2 * features), BF16),
            pltpu.VMEM((2 * features, nodes), BF16),
            pltpu.SemaphoreType.DMA((2 * blocks + 2,)),
            pltpu.SemaphoreType.DMA((4,)),
        ],
        FORWARD,
        "forward",
        60,
    )


def fetch_kernel(distance, group_ref, k_below, k_above, v_below, v_above, match_ref, found_ref, rows, sems):
    nodes, both = rows.shape
    features = both // 2
    lanes = (pl.ds(0, features), pl.ds(features, features))
    copies = []
    below_is_partner = lax.rem(group_ref[0] // distance, 2) == 1
    for which, (below, above) in enumerate(((k_below, k_above), (v_below, v_above))):
        target = rows.at[:, lanes[which]]

        @pl.when(below_is_partner)
        def _():
            pltpu.make_async_copy(below, target, sems.at[which]).start()

        @pl.when(jnp.logical_not(below_is_partner))
        def _():
            pltpu.make_async_copy(above, target, sems.at[which]).start()

        copies.append(pltpu.make_async_copy(below, target, sems.at[which]))
    target_node = lax.broadcasted_iota(jnp.int32, (nodes, nodes), 0)
    chosen = (target_node == match_ref[...]).astype(F32).astype(BF16)
    for copy in copies:
        copy.wait()
    found_ref[...] = dot(rows[...], chosen, ROWS_DOWN).astype(BF16)


def fetch(distance, group, arrays, match_row):
    nodes = match_row.shape[1]
    features = arrays[0].shape[1]
    return run(
        functools.partial(fetch_kernel, distance),
        (group,),
        [(array, ANYWHERE) for array in arrays] + [(match_row, None)],
        [((2 * features, nodes), BF16)],
        [pltpu.VMEM((nodes, 2 * features), BF16), pltpu.SemaphoreType.DMA((4,))],
        FETCH,
        "fetch",
        60,
    )[0]


def place_kernel(match_ref, rows_ref, *placed):
    nodes = match_ref.shape[1]
    target_node = lax.broadcasted_iota(jnp.int32, (nodes, nodes), 0)
    for turn, placed_ref in enumerate(placed):
        chosen = (target_node == match_ref[turn : turn + 1, :]).astype(F32).astype(BF16)
        placed_ref[...] = dot(rows_ref[turn].astype(BF16), chosen, ROWS_ACROSS)


def place(matching, rows):
    out = (rows.shape[1:], F32)
    return run(place_kernel, (), [(matching, None), (rows, None)], [out] * 3, [], PLACE, "place", 60)


def backward(half, scalars, key_rows, value_rows, halo, query_rows, attended_grad, stats, edge_part, spare, heads):
    tile_block, tile_count = scalars
    nodes, features = query_rows.shape
    blocks, slots = tile_count.shape[0], tile_block.shape[0] // tile_count.shape[0]
    per, width = nodes // blocks, features // 2
    columns = heads // 2 * per
    count = halo.shape[0]
    part = pl.BlockSpec((nodes, width), lambda *_: (0, half), pipeline_mode=pl.Buffered(1))
    return run(
        functools.partial(backward_kernel, half, heads // 2, features // heads),
        scalars,
        [(key_rows, ANYWHERE), (value_rows, ANYWHERE), (halo, ANYWHERE), (query_rows, part)]
        + [(attended_grad, part), (stats, None), (edge_part, None)],
        [
            ((count, per + spare, features), BF16),
            ((blocks, per, features), F32),
            ((nodes, width), F32),
        ],
        [
            pltpu.VMEM((blocks + count, per, features), BF16),
            pltpu.VMEM((1, slots * per, features), BF16),
            pltpu.VMEM((1, slots * per, columns), BF16),
            pltpu.VMEM((1, slots * per, columns), BF16),
            pltpu.VMEM((blocks + count, per, features), F32),
            pltpu.VMEM((count, per, features), BF16),
            pltpu.SemaphoreType.DMA((2 * blocks + 2,)),
            pltpu.SemaphoreType.DMA((9,)),
        ],
        BACKWARD,
        "backward",
        60,
        (0, 1),
    )


def add_home(send_block, home_ref, key_ref, value_ref, width):
    per = home_ref.shape[1]
    for slot in range(home_ref.shape[0]):
        rows = pl.ds(pl.multiple_of(send_block[slot] * per, per), per)
        key_ref[rows, :width] += home_ref[slot, :, :width].astype(F32)
        value_ref[rows, :width] += home_ref[slot, :, width:].astype(F32)


def collect_kernel(heads, send_block, own_a, own_b, home_ref, *refs):
    placed, edges = refs[:3], refs[3:6]
    key_ref, value_ref = refs[6:]
    blocks, per, two = own_a.shape
    width = two // 2
    dim = width // heads
    for block in range(blocks):
        at = slice(block * per, (block + 1) * per)
        key_ref[at, :width] = own_a[block, :, :width]
        key_ref[at, width:] = own_b[block, :, :width]
        value_ref[at, :width] = own_a[block, :, width:]
        value_ref[at, width:] = own_b[block, :, width:]
    row = lax.broadcasted_iota(jnp.int32, (4 * heads, two), 0)
    lane = lax.broadcasted_iota(jnp.int32, (4 * heads, two), 1)
    key_row = (lane // width) * (2 * heads) + lax.rem(lane, width) // dim
    key_spread = (row == key_row).astype(F32).astype(BF16)
    value_spread = (row == key_row + heads).astype(F32).astype(BF16)
    for turn in range(3):
        scalars = edges[turn][...].astype(BF16)
        dscore = dot(scalars, key_spread, ROWS_DOWN)
        weight = dot(scalars, value_spread, ROWS_DOWN)
        key_term = dscore * placed[turn][:, :two].astype(F32)
        value_term = weight * placed[turn][:, two:].astype(F32)
        key_ref[...] += key_term.astype(BF16).astype(F32)
        value_ref[...] += value_term.astype(BF16).astype(F32)
    add_home(send_block, home_ref, key_ref, value_ref, width)


def collect(send_block, own_a, own_b, home, placed, edges, heads):
    blocks, per, two = own_a.shape
    slots = home.shape[0]
    out = ((blocks * per, two), F32)
    part = pl.BlockSpec((slots, per, two), lambda *_: (0, 0, 0), pipeline_mode=pl.Buffered(1))
    return run(
        functools.partial(collect_kernel, heads // 2),
        (send_block,),
        [(own_a, None), (own_b, None), (home, part)] + [(array, None) for array in (*placed, *edges)],
        [out, out],
        [],
        COLLECT,
        "collect",
        60,
    )


def finish_kernel(send_block, home_ref, key_in, value_in, key_ref, value_ref):
    key_ref[...] = key_in[...]
    value_ref[...] = value_in[...]
    add_home(send_block, home_ref, key_ref, value_ref, key_ref.shape[1])


def finish(send_block, home, key_sum, value_sum):
    nodes, two = key_sum.shape
    half = pl.BlockSpec((nodes, two // 2), lambda *_: (0, 1), pipeline_mode=pl.Buffered(1))
    return pl.pallas_call(
        finish_kernel,
        grid_spec=pltpu.PrefetchScalarGridSpec(
            num_scalar_prefetch=1,
            grid=(1,),
            in_specs=[whole(home.shape), half, half],
            out_specs=[half, half],
        ),
        out_shape=[jax.ShapeDtypeStruct((nodes, two), F32)] * 2,
        input_output_aliases={2: 0, 3: 1},
        compiler_params=params(),
        cost_estimate=cost(FINISH, 1 << 10),
        name="finish",
    )(send_block, home, key_sum, value_sum)


def from_partner(array, apart):
    axes = ("group", "dom")
    return lax.ppermute(array, axes, [(i, i ^ 1 << apart) for i in range(lax.axis_size(axes))])


def ahead(array, steps):
    count = lax.axis_size("group")
    return lax.ppermute(array, "group", [(i, (i + steps) % count) for i in range(count)])


def across(array, axis, apart):
    return lax.ppermute(array, axis, [(i, i ^ apart) for i in range(lax.axis_size(axis))])


def exchange(array, axis):
    return lax.all_to_all(array, axis, split_axis=0, concat_axis=0, tiled=True)


def shards(
    query_rows,
    key_rows,
    value_rows,
    out_weight,
    grad_update,
    expander_bias,
    tile_block,
    tile_count,
    send_block,
    matching,
):
    nodes, features = query_rows.shape
    heads = expander_bias.shape[0]
    tile_block = tile_block[0]
    tile_count = tile_count[0]
    send_block = send_block[0]
    matching = matching[0]
    per = nodes // tile_block.shape[0]
    devices = lax.axis_size(("group", "dom"))
    top_bit = devices.bit_length() - 1
    groups = lax.axis_size("group")

    halo = exchange(outgoing(send_block, key_rows, value_rows, per), "dom")
    attended_grad, *placed = prepare(query_rows, grad_update, out_weight, matching)
    half = nodes // 2
    near = [(ahead(rows, 1), ahead(rows, -1)) for rows in (key_rows, value_rows)]
    near[0], attended_grad = lax.optimization_barrier((near[0], attended_grad))
    group = lax.axis_index("group").astype(jnp.int32).reshape(1)

    def found(turn, distance, ring):
        return fetch(distance, group, [rows for pair in ring for rows in pair], matching[turn : turn + 1])

    next_near = [(ahead(below, 1), ahead(above, -1)) for below, above in near]
    far_2 = found(2, 1, near)
    next_near[1], far_2 = lax.optimization_barrier((next_near[1], far_2))
    third = [(ahead(below[:half], 1), ahead(above[half:], -1)) for below, above in next_near]
    fourth = [(ahead(below, 1), ahead(above, -1)) for below, above in third]
    far_1 = found(1, 2, next_near)
    fourth, far_1, placed[0] = lax.optimization_barrier((fourth, far_1, placed[0]))
    placed = [from_partner(placed[turn], top_bit - 1 - turn) for turn in range(3)]
    fourth = [rows for pair in fourth for rows in pair]

    scalars = (tile_block.reshape(-1), tile_count)
    update, pieces, stats, edge_part, edges = forward(
        scalars, expander_bias, halo, fourth, matching[:1], (far_1, far_2), key_rows, value_rows, query_rows,
        attended_grad, grad_update, out_weight,
    )
    pieces = exchange(pieces, "group")
    spare = features // groups
    common = (scalars, key_rows, value_rows, halo, query_rows, attended_grad)
    back_a, own_a, query_a = backward(0, *common, stats, edge_part, spare, heads)
    part = pieces.astype(F32).sum(axis=0).astype(BF16)
    back_a = back_a.at[:, per:, :].set(part[None])
    back_a, placed[0] = lax.optimization_barrier((back_a, placed[0]))
    home_a = exchange(back_a, "dom")
    back_b, own_b, query_b = backward(1, *common, stats, edge_part, 0, heads)
    edges = place(matching, edges)
    back_b, home_a, placed[1], placed[2], *edges = lax.optimization_barrier(
        (back_b, home_a, placed[1], placed[2], *edges)
    )
    edges = [from_partner(edges[turn], top_bit - 1 - turn) for turn in range(3)]
    home_b = exchange(back_b, "dom")
    query_grad = jnp.concatenate([query_a, query_b], axis=1)

    weight_grad = home_a[:, per:, :].astype(F32).sum(axis=0) * (nodes * devices) ** (-0.5)
    apart = 1
    while apart < groups:
        other = across(weight_grad, "group", apart)
        upper = lax.rem(group[0] // apart, 2) == 1
        weight_grad = jnp.where(
            upper, jnp.concatenate([other, weight_grad]), jnp.concatenate([weight_grad, other])
        )
        apart *= 2
    key_sum, value_sum = collect(send_block, own_a, own_b, home_a, placed, edges, heads)
    home_b, key_sum, value_sum, weight_grad, query_grad = lax.optimization_barrier(
        (home_b, key_sum, value_sum, weight_grad, query_grad)
    )
    key_grad, value_grad = finish(send_block, home_b, key_sum, value_sum)
    return (update, query_grad, key_grad, value_grad, weight_grad)


def solution(mesh):
    rows = P(("group", "dom"), None)
    in_specs = (
        rows,
        rows,
        rows,
        P(),
        rows,
        P(),
        P(("group", "dom"), None, None),
        rows,
        rows,
        P(("group", "dom"), None, None),
    )
    out_specs = (rows, rows, rows, rows, P())
    return jax.shard_map(shards, mesh=mesh, in_specs=in_specs, out_specs=out_specs, check_vma=False)
```
